256 devices in a mesh: qa: 32 (over y, z_lo, core), qb: 8 (over z_hi, x).
Axes of the slice: x: 4, y: 4, z: 8 (z_hi: 2, z_lo: 4; z = z_hi * 4 + z_lo), core: 2. Of those that a mesh axis runs over, the one named last changes fastest.
Arguments:
- amplitudes: float32 [2, 16777216], P(None, ('qa', 'qb')), may hold values from -6 to 6
- gate_mats: float32 [6, 2, 128, 128], replicated, may hold values from -0.375 to 0.375
- gate_order: int32 [6, 7], replicated, may hold values from 0 to 6, each once within a row
- phase_pairs: int32 [3, 4, 2], replicated, may hold values from 0 to 23
- phase_angles: float32 [3, 4], replicated, may hold values from -3.140625 to 3.140625
Outputs:
- evolved: float32 [2, 16777216], P(None, ('qa', 'qb'))
The draws below stay inside these ranges and needn't reach their ends.
Inputs may be any that keep to these rules, and one draw needn't show every extreme that they name: `gate_order`: each row is an order of the 7 qubits of one merged gate. `phase_pairs`: qubit numbers below 24; the two of a coupling may coincide.
All inputs are finite; a program needn't handle non-finite values.
Results may differ from the reference program's by a relative error of at most 0.0001.
Values sent between devices are 32-bit elements; how exact they have to be, the bound alone decides.
No kernel may reach another device: no remote copies, remote signals or barrier semaphores. Data moves between devices by JAX's collectives and lax.ppermute only.
A program may use at most 64 MiB of HBM per device.

```python
import jax
import jax.numpy as jnp
from jax import lax

GATE_QUBITS = 7
LAYERS = 3
PHASES = 4
MERGED = 128
A_HIGH = 4
B_LOW = 16
LOCAL = 65536
AMPLITUDE_TOTAL = 16777216
GATES = 6
QUBITS = 24
N_QA = 32
N_QB = 8


def set_ends(drawn, own_key, low, high):
    longest = drawn.shape.index(max(drawn.shape))
    spots = []
    for shift in (0, 1):
        where = [jax.random.randint(jax.random.fold_in(own_key, axis), (), 0, length) for axis, length in enumerate(drawn.shape)]
        where[longest] = (where[longest] + shift) % drawn.shape[longest]
        spots.append(tuple(where))
    return drawn.at[spots[0]].set(low).at[spots[1]].set(high)


def level_of(stream_key, dims, split, least, high):
    factor_of = 1.0
    for dim, shards_of in split:
        heights = jax.random.uniform(jax.random.fold_in(jax.random.fold_in(stream_key, 6), dim), (shards_of,), jnp.float32, least / len(split), high / len(split))
        factor_of = factor_of * jnp.repeat(jnp.exp(heights), dims[dim] // shards_of).reshape((-1,) + (1,) * (len(dims) - 1 - dim))
    return factor_of


def bell_draw(stream_key, extent, scale, bound, cuts=(), kind=jnp.bfloat16):
    level = level_of(stream_key, extent, cuts, -0.22, 0.18) if cuts else 1.0
    array = jax.random.normal(stream_key, extent, jnp.float32) * scale * level
    return jnp.minimum(jnp.maximum(array, -bound), bound).astype(kind)


def setup_inputs(seed: int = 0) -> dict:
    keys = jax.random.split(jax.random.key(seed), 6)
    return {
        "amplitudes": bell_draw(keys[0], (2, AMPLITUDE_TOTAL), 1.0, 6.0, ((1, 256),), jnp.float32),
        "gate_mats": bell_draw(keys[1], (GATES, 2, MERGED, MERGED), (2 * MERGED) ** -0.5, 0.375, (), jnp.float32),
        "gate_order": jax.vmap(lambda own: jax.random.permutation(own, GATE_QUBITS))(jax.random.split(keys[2], GATES)).reshape((GATES, GATE_QUBITS)).astype(jnp.int32),
        "phase_pairs": set_ends(jax.random.randint(keys[3], (LAYERS, PHASES, 2), 0, QUBITS), jax.random.fold_in(keys[3], 1), 0, QUBITS - 1).astype(jnp.int32),
        "phase_angles": jnp.clip(jax.random.uniform(keys[4], (LAYERS, PHASES), jnp.float32, -3.140625, 3.140625), -3.140625, 3.140625),
    }


def effective(gate_mats, gate_order):
    column = jnp.arange(MERGED, dtype=jnp.int32)
    matrices = []
    for gate_idx in range(GATES):
        mapped = jnp.zeros((MERGED,), jnp.int32)
        for qubit_pos in range(GATE_QUBITS):
            picked_bit = jnp.bitwise_and(jnp.right_shift(column, gate_order[gate_idx, qubit_pos]), 1)
            mapped = mapped + jnp.left_shift(picked_bit, qubit_pos)
        chosen = gate_mats[gate_idx][:, mapped][:, :, mapped]
        matrices.append(chosen)
    return matrices


def rotate_phases(amp_values, pairs, angles):
    index_all = jnp.arange(AMPLITUDE_TOTAL, dtype=jnp.int32)
    phase_sum = jnp.zeros((AMPLITUDE_TOTAL,), jnp.float32)
    for term_idx in range(PHASES):
        first_bit = jnp.bitwise_and(jnp.right_shift(index_all, pairs[term_idx, 0]), 1)
        second_bit = jnp.bitwise_and(jnp.right_shift(index_all, pairs[term_idx, 1]), 1)
        sign_value = (1.0 - 2.0 * first_bit.astype(jnp.float32)) * (1.0 - 2.0 * second_bit.astype(jnp.float32))
        phase_sum = phase_sum + angles[term_idx] * sign_value
    cosine = jnp.cos(phase_sum)
    sine_part = jnp.sin(phase_sum)
    real_part = amp_values[0]
    imag_part = amp_values[1]
    return jnp.stack([real_part * cosine - imag_part * sine_part, real_part * sine_part + imag_part * cosine])


def complex_blend(pattern, matrix, amp_values):
    def product(left, right):
        return jnp.einsum(pattern, left, right, precision=lax.Precision.HIGHEST)
    real_out = product(matrix[0], amp_values[0]) - product(matrix[1], amp_values[1])
    imag_out = product(matrix[0], amp_values[1]) + product(matrix[1], amp_values[0])
    return jnp.stack([real_out, imag_out])


def reference(amplitudes, gate_mats, gate_order, phase_pairs, phase_angles):
    matrices = effective(gate_mats, gate_order)
    present_state = amplitudes
    for layer_idx in range(LAYERS):
        present_state = rotate_phases(present_state, phase_pairs[layer_idx], phase_angles[layer_idx])
        outer_gate = matrices[2 * layer_idx]
        central_gate = matrices[2 * layer_idx + 1]
        if layer_idx % 2 == 0:
            reshaped_state = present_state.reshape(2, N_QA, N_QB, A_HIGH, LOCAL // A_HIGH)
            gate_four = outer_gate.reshape(2, A_HIGH, N_QA, A_HIGH, N_QA)
            present_state = complex_blend('pqst,tbsr->qbpr', gate_four, reshaped_state).reshape(2, AMPLITUDE_TOTAL)
            reshaped_state = present_state.reshape(2, AMPLITUDE_TOTAL // MERGED, MERGED)
            present_state = complex_blend('km,pm->pk', central_gate, reshaped_state).reshape(2, AMPLITUDE_TOTAL)
        else:
            reshaped_state = present_state.reshape(2, N_QA, N_QB, LOCAL // MERGED, N_QB, B_LOW)
            gate_four = outer_gate.reshape(2, N_QB, B_LOW, N_QB, B_LOW)
            present_state = complex_blend('pqst,asbyt->apbyq', gate_four, reshaped_state).reshape(2, AMPLITUDE_TOTAL)
            reshaped_state = present_state.reshape(2, N_QA * N_QB, MERGED, LOCAL // MERGED)
            present_state = complex_blend('db,ebj->edj', central_gate, reshaped_state).reshape(2, AMPLITUDE_TOTAL)
    return present_state
```

```python
import itertools

import jax
import jax.numpy as jnp
from jax import lax
from jax.experimental import pallas as pl
from jax.experimental.pallas import tpu as pltpu
from jax.sharding import PartitionSpec as P

AXES = ("qa", "qb")
SIZES = {"y": 4, "zl": 4, "c": 2, "zh": 2, "x": 4}
F32 = jnp.float32
BF16 = jnp.bfloat16
LANES = 128


def device_groups(varying):
    fixed = [name for name in SIZES if name not in varying]
    groups = []
    for held in itertools.product(*[range(SIZES[name]) for name in fixed]):
        group = []
        for moved in itertools.product(*[range(SIZES[name]) for name in varying]):
            at = dict(zip(fixed, held)) | dict(zip(varying, moved))
            group.append((at["y"] * 8 + at["zl"] * 2 + at["c"]) * 8 + at["zh"] * 4 + at["x"])
        groups.append(group)
    return groups


def exchange(values, varying):
    groups = device_groups(varying)
    parts = values.reshape(len(groups[0]), -1, LANES)
    if len(groups) == 1:
        moved = lax.all_to_all(parts, AXES, 0, 0, tiled=True)
    else:
        moved = lax.all_to_all(parts, AXES, 0, 0, axis_index_groups=groups, tiled=True)
    return moved.reshape(values.shape)


def iota(axis, shape=(128, 128)):
    return lax.broadcasted_iota(jnp.int32, shape, axis)


def take_bits(index, places):
    total = None
    for source, place in enumerate(places):
        bit = jnp.left_shift(jnp.bitwise_and(jnp.right_shift(index, source), 1), place)
        total = bit if total is None else total + bit
    return total


def onehot(order_ref, gate, places, axis):
    index = take_bits(iota(axis), places)
    mapped = None
    for target in range(7):
        bit = jnp.bitwise_and(jnp.right_shift(index, order_ref[gate, target]), 1)
        bit = jnp.left_shift(bit, target)
        mapped = bit if mapped is None else mapped + bit
    return (mapped == iota(1 - axis)).astype(F32).astype(BF16)


def mul(left, right):
    return jnp.dot(left, right, preferred_element_type=F32)


def mul_t(left, right):
    return lax.dot_general(left, right, (((1,), (1,)), ((), ())), preferred_element_type=F32)


def halves(values):
    high = values.astype(BF16)
    return high, (values - high.astype(F32)).astype(BF16)


NATURAL = tuple(range(7))


def gate_block(mats_ref, order_ref, gate, row_places=NATURAL, column_places=NATURAL):
    rows = onehot(order_ref, gate, row_places, 0)
    columns = onehot(order_ref, gate, column_places, 1)
    blocks = []
    real, imag = [halves(mats_ref[gate, part]) for part in range(2)]
    for real_half, imag_half in zip(real, imag):
        both = jnp.concatenate([real_half, imag_half], axis=0)
        both = mul(both, columns).astype(BF16)
        vr = mul(rows, both[:128]).astype(BF16)
        vi = mul(rows, both[128:]).astype(BF16)
        blocks.append((vr, vi))
    return blocks


def full_block(blocks):
    out = []
    for vr, vi in blocks:
        out.append(
            jnp.concatenate(
                [jnp.concatenate([vr, -vi], axis=1), jnp.concatenate([vi, vr], axis=1)], axis=0
            )
        )
    return out


def product(multiply, block, values, values_left=False):
    high, low = halves(values)
    block_high, block_low = block
    if values_left:
        return multiply(high, block_high) + (multiply(low, block_high) + multiply(high, block_low))
    return multiply(block_high, high) + (multiply(block_high, low) + multiply(block_low, high))


def sign_of(index, pairs_ref, layer, term):
    first = jnp.right_shift(index, pairs_ref[layer, term, 0])
    second = jnp.right_shift(index, pairs_ref[layer, term, 1])
    bit = jnp.bitwise_and(jnp.bitwise_xor(first, second), 1)
    return (1 - 2 * bit).astype(F32)


class Phase:
    def __init__(self, pairs_ref, angles_ref, layer, index):
        self.pairs_ref = pairs_ref
        self.layer = layer
        angles = angles_ref[...]
        cosine = jnp.cos(angles)
        sine = jnp.sin(angles)
        self.cosine = [cosine[layer : layer + 1, term : term + 1] for term in range(4)]
        self.sine = [
            sine[layer : layer + 1, term : term + 1] * sign_of(index, pairs_ref, layer, term)
            for term in range(4)
        ]

    def __call__(self, real, imag, rest):
        factors = []
        for term in range(4):
            sign = sign_of(rest, self.pairs_ref, self.layer, term)
            factors.append((self.cosine[term], self.sine[term] * sign))

        def pair(first, second):
            return (
                first[0] * second[0] - first[1] * second[1],
                first[0] * second[1] + first[1] * second[0],
            )

        cosine, sine = pair(pair(factors[0], factors[1]), pair(factors[2], factors[3]))
        return real * cosine - imag * sine, real * sine + imag * cosine


def swap_bit(tiles, tile_bit, lane_bit):
    width = 1 << lane_bit
    lane = iota(1, tiles[0].shape)
    low = jnp.bitwise_and(lane, width) == 0
    out = list(tiles)
    for number in range(len(tiles)):
        other = number | (1 << tile_bit)
        if other == number:
            continue
        first, second = tiles[number], tiles[other]
        out[number] = jnp.where(low, first, pltpu.roll(second, width, 1))
        out[other] = jnp.where(low, pltpu.roll(first, LANES - width, 1), second)
    return out


def place():
    qa = lax.axis_index("qa")
    qb = lax.axis_index("qb")
    return qa // 2, qa % 2, qb // 4, qb % 4


def kernel_a(amps_ref, mats_ref, order_ref, pairs_ref, angles_ref, out_ref):
    block = full_block(gate_block(mats_ref, order_ref, 1))
    yz, core, zh, x = place()
    device = yz * (1 << 20) + core * (1 << 19) + zh * (1 << 18) + x * (1 << 16)
    phase = Phase(pairs_ref, angles_ref, 0, iota(0) * 512 + iota(1))
    for mid in range(4):
        real = amps_ref[pl.ds(2 * mid, 128, stride=8), :]
        imag = amps_ref[pl.ds(2 * mid + 1, 128, stride=8), :]
        real, imag = phase(real, imag, device + mid * 128)
        values = jnp.concatenate([real, imag], axis=1)
        result = product(mul_t, block, values)
        for part in range(2):
            tiles = result[part * 128 : (part + 1) * 128].reshape(16, 8, LANES)
            out_ref[mid * 16 : (mid + 1) * 16, part * 8 : (part + 1) * 8, :] = tiles


def kernel_b(amps_ref, mats_ref, order_ref, pairs_ref, angles_ref, out_ref):
    yz, core, zh, x = place()
    device = yz * (1 << 4) + core * (1 << 3) + zh * (1 << 8) + x * (1 << 16)
    block_0 = full_block(gate_block(mats_ref, order_ref, 0))
    columns = []
    for u in range(4):
        parts = []
        for part in range(2):
            start = (u // 2) * 512 + part * 8 + (u % 2) * 4
            tiles = [amps_ref[pl.ds(start + t, 32, stride=16), :] for t in range(4)]
            tiles = swap_bit(swap_bit(tiles, 1, 6), 0, 5)
            parts += tiles
        columns.append(jnp.concatenate(parts, axis=0))
    result = product(mul, block_0, jnp.concatenate(columns, axis=1))
    row, lane = iota(0), iota(1)
    index = (row // 32) * (1 << 14) + (row % 32) * (1 << 19) + (lane // 32) + (lane % 32) * 512
    phase = Phase(pairs_ref, angles_ref, 1, index)
    block_3 = gate_block(mats_ref, order_ref, 3)
    block_3 = [
        jnp.concatenate(
            [
                jnp.concatenate([vr, -vi], axis=1).reshape(32, 4, 256),
                jnp.concatenate([vi, vr], axis=1).reshape(32, 4, 256),
            ],
            axis=1,
        ).reshape(256, 256)
        for vr, vi in [(vr.astype(F32), vi.astype(F32)) for vr, vi in block_3]
    ]
    block_3 = [half.astype(BF16) for half in block_3]
    rows = []
    for u in range(4):
        real = result[:128, u * 128 : (u + 1) * 128]
        imag = result[128:, u * 128 : (u + 1) * 128]
        parts = []
        for value in phase(real, imag, device + (u // 2) * (1 << 18) + (u % 2) * 4):
            tiles = [value[ah * 32 : (ah + 1) * 32] for ah in range(4)]
            tiles = swap_bit(swap_bit(tiles, 1, 6), 0, 5)
            parts.append(jnp.concatenate(tiles, axis=0))
        rows.append(jnp.concatenate(parts, axis=1))
    result = product(mul_t, block_3, jnp.concatenate(rows, axis=0))
    for u in range(4):
        values = result[:, u * 128 : (u + 1) * 128]
        tiles = [values[ah * 64 : (ah + 1) * 64] for ah in range(4)]
        tiles = swap_bit(swap_bit(tiles, 1, 6), 0, 5)
        for t in range(4):
            out_ref[:, u * 4 + t, :, :] = tiles[t].reshape(8, 8, LANES)


def kernel_c(amps_ref, mats_ref, order_ref, pairs_ref, angles_ref, out_ref):
    yz, core, zh, x = place()
    device = yz * (1 << 4) + core * (1 << 11) + zh * (1 << 8) + x * (1 << 12)
    block_2 = full_block(gate_block(mats_ref, order_ref, 2, NATURAL, (0, 1, 2, 6, 3, 4, 5)))
    columns = []
    for xl in range(4):
        columns.append(
            jnp.concatenate(
                [amps_ref[pl.ds(part * 4 + xl, 128, stride=8), :] for part in range(2)], axis=0
            )
        )
    result = product(mul, block_2, jnp.concatenate(columns, axis=1))
    row, lane = iota(0), iota(1)
    index = (row // 16) * (1 << 16) + (row % 16) + (lane // 32) * (1 << 14) + (lane % 32) * (1 << 19)
    phase = Phase(pairs_ref, angles_ref, 2, index)
    block_4 = full_block(gate_block(mats_ref, order_ref, 4))
    rotated = [
        phase(
            result[:128, xl * 128 : (xl + 1) * 128],
            result[128:, xl * 128 : (xl + 1) * 128],
            device + xl * 512,
        )
        for xl in range(4)
    ]
    rows = []
    for gb in range(8):
        for xl in range(4):
            real, imag = rotated[xl]
            rows.append(
                jnp.concatenate(
                    [real[gb * 16 : (gb + 1) * 16], imag[gb * 16 : (gb + 1) * 16]], axis=1
                )
            )
    result = product(mul_t, block_4, jnp.concatenate(rows, axis=0))
    for pair in range(4):
        values = result[:, pair * 128 : (pair + 1) * 128]
        tiles = swap_bit([values[:128], values[128:]], 0, 6)
        for last in range(2):
            gb = pair * 2 + last
            for ah in range(4):
                out_ref[pl.ds(gb * 4 + ah, 32, stride=32), :] = tiles[last][ah * 32 : (ah + 1) * 32]


def kernel_d(amps_ref, mats_ref, order_ref, out_ref):
    block = full_block(gate_block(mats_ref, order_ref, 5))
    rows = []
    for b7 in range(2):
        start = b7 * 512
        tiles = [amps_ref[start + xb * 64 : start + (xb + 1) * 64, :] for xb in range(8)]
        tiles = swap_bit(swap_bit(swap_bit(tiles, 2, 6), 1, 5), 0, 4)
        for xl in range(4):
            rows.append(jnp.concatenate([tiles[xl], tiles[4 + xl]], axis=1))
    result = product(mul_t, block, jnp.concatenate(rows, axis=0), values_left=True)
    for b7 in range(2):
        for xl in range(4):
            start = (b7 * 4 + xl) * 64
            for b11, b8, b13, b12 in itertools.product(range(2), repeat=4):
                at = start + b11 * 32 + b8 * 16 + b13 * 8 + b12 * 4
                to = b13 * 64 + b12 * 32 + b11 * 16 + xl * 4 + b8 * 2 + b7
                for part in range(2):
                    out_ref[pl.ds(2 * to + part, 4, stride=256), :] = result[
                        at : at + 4, part * 128 : (part + 1) * 128
                    ]


def call(kernel, name, shape, operands, scalars):
    return pl.pallas_call(
        kernel,
        out_shape=jax.ShapeDtypeStruct(shape, F32),
        in_specs=[pl.BlockSpec(memory_space=pltpu.VMEM)] * 2
        + [pl.BlockSpec(memory_space=pltpu.SMEM)] * (scalars if scalars < 2 else 2)
        + ([pl.BlockSpec(memory_space=pltpu.VMEM)] if scalars > 2 else []),
        out_specs=pl.BlockSpec(memory_space=pltpu.VMEM),
        compiler_params=pltpu.CompilerParams(vmem_limit_bytes=24 * 1024 * 1024),
        cost_estimate=pl.CostEstimate(flops=400_000_000, bytes_accessed=2_000_000, transcendentals=0),
        name=name,
    )(*operands)


def body(amplitudes, gate_mats, gate_order, phase_pairs, phase_angles):
    shared = (gate_mats, gate_order, phase_pairs, phase_angles)
    state = amplitudes.reshape(2, 512, LANES).transpose(1, 0, 2).reshape(1024, LANES)
    state = call(kernel_a, "first_gate", (64, 16, LANES), (state, *shared), 3)
    state = exchange(state, ["zh", "y", "zl", "c"]).reshape(1024, LANES)
    state = call(kernel_b, "second_gates", (8, 16, 8, LANES), (state, *shared), 3)
    state = exchange(state.reshape(1024, LANES), ["x", "c"])
    state = call(kernel_c, "third_gates", (1024, LANES), (state, *shared), 3)
    state = exchange(state, ["y", "zl", "c", "zh", "x"])
    state = call(kernel_d, "last_gate", (1024, LANES), (state, gate_mats, gate_order), 1)
    return state.reshape(512, 2, LANES).transpose(1, 0, 2).reshape(2, 65536)


def solution(mesh):
    return jax.shard_map(
        body,
        mesh=mesh,
        in_specs=(P(None, AXES), P(), P(), P(), P()),
        out_specs=P(None, AXES),
        check_vma=False,
    )
```

```python
import itertools

import jax
import jax.numpy as jnp
from jax import lax
from jax.experimental import pallas as pl
from jax.experimental.pallas import tpu as pltpu
from jax.sharding import PartitionSpec as P

AXES = ("qa", "qb")
SIZES = {"y": 4, "zl": 4, "c": 2, "zh": 2, "x": 4}
F32 = jnp.float32
BF16 = jnp.bfloat16
LANES = 128


def device_groups(varying):
    fixed = [name for name in SIZES if name not in varying]
    groups = []
    for held in itertools.product(*[range(SIZES[name]) for name in fixed]):
        group = []
        for moved in itertools.product(*[range(SIZES[name]) for name in varying]):
            at = dict(zip(fixed, held)) | dict(zip(varying, moved))
            group.append((at["y"] * 8 + at["zl"] * 2 + at["c"]) * 8 + at["zh"] * 4 + at["x"])
        groups.append(group)
    return groups


def exchange(values, varying):
    groups = device_groups(varying)
    parts = values.reshape(len(groups[0]), -1, LANES)
    if len(groups) == 1:
        moved = lax.all_to_all(parts, AXES, 0, 0, tiled=True)
    else:
        moved = lax.all_to_all(parts, AXES, 0, 0, axis_index_groups=groups, tiled=True)
    return moved.reshape(values.shape)


def iota(axis, shape=(128, 128)):
    return lax.broadcasted_iota(jnp.int32, shape, axis)


def take_bits(index, places):
    total = None
    for source, place in enumerate(places):
        bit = jnp.left_shift(jnp.bitwise_and(jnp.right_shift(index, source), 1), place)
        total = bit if total is None else total + bit
    return total


def onehot(order_ref, gate, index):
    mapped = None
    order = order_ref[...]
    for target in range(7):
        shift = order[gate : gate + 1, target : target + 1]
        bit = jnp.bitwise_and(jnp.right_shift(index, shift), 1)
        bit = jnp.left_shift(bit, target)
        mapped = bit if mapped is None else mapped + bit
    return (mapped == iota(1)).astype(F32).astype(BF16)


def mul(left, right):
    return jnp.dot(left, right, preferred_element_type=F32)


def mul_t(left, right):
    return lax.dot_general(left, right, (((1,), (1,)), ((), ())), preferred_element_type=F32)


def halves(values):
    high = values.astype(BF16)
    return high, (values - high.astype(F32)).astype(BF16)


def gate_block(mats, order_ref, gate, rows=None, columns=None):
    rows = onehot(order_ref, gate, iota(0) if rows is None else rows)
    columns = rows if columns is None else onehot(order_ref, gate, columns)
    parts = [half for part in range(2) for half in halves(mats[part])]
    turned = mul_t(columns, jnp.concatenate(parts, axis=0)).astype(BF16)
    parts = [mul_t(rows, turned[:, at * 128 : (at + 1) * 128]).astype(BF16) for at in range(4)]
    return [(parts[0], parts[2]), (parts[1], parts[3])]


def full_block(blocks):
    out = []
    for vr, vi in blocks:
        out.append(
            jnp.concatenate(
                [jnp.concatenate([vr, -vi], axis=1), jnp.concatenate([vi, vr], axis=1)], axis=0
            )
        )
    return out


def product(multiply, block, values, values_left=False):
    high, low = halves(values)
    block_high, block_low = block
    if values_left:
        return multiply(high, block_high) + (multiply(low, block_high) + multiply(high, block_low))
    return multiply(block_high, high) + (multiply(block_high, low) + multiply(block_low, high))


def sign_of(index, pairs, layer, term):
    first = jnp.right_shift(index, pairs[layer, 0:1, term : term + 1])
    second = jnp.right_shift(index, pairs[layer, 1:2, term : term + 1])
    bit = jnp.bitwise_and(jnp.bitwise_xor(first, second), 1)
    return (1 - 2 * bit).astype(F32)


class Phase:
    def __init__(self, pairs_ref, angles_ref, layer, index):
        self.pairs = pairs_ref[...]
        self.layer = layer
        angles = angles_ref[...]
        cosine = jnp.cos(angles)
        sine = jnp.sin(angles)
        self.cosine = [cosine[layer : layer + 1, term : term + 1] for term in range(4)]
        self.sine = [
            sine[layer : layer + 1, term : term + 1] * sign_of(index, self.pairs, layer, term)
            for term in range(4)
        ]

    def factor(self, rest):
        rest = jnp.full((1, 1), rest, jnp.int32)
        factors = []
        for term in range(4):
            sign = sign_of(rest, self.pairs, self.layer, term)
            factors.append((self.cosine[term], self.sine[term] * sign))

        def pair(first, second):
            return (
                first[0] * second[0] - first[1] * second[1],
                first[0] * second[1] + first[1] * second[0],
            )

        return pair(pair(factors[0], factors[1]), pair(factors[2], factors[3]))


def rotate(factor, real, imag):
    cosine, sine = factor
    return real * cosine - imag * sine, real * sine + imag * cosine


def swap_bit(tiles, tile_bit, lane_bit):
    width = 1 << lane_bit
    lane = iota(1, tiles[0].shape)
    low = jnp.bitwise_and(lane, width) == 0
    out = list(tiles)
    for number in range(len(tiles)):
        other = number | (1 << tile_bit)
        if other == number:
            continue
        first, second = tiles[number], tiles[other]
        out[number] = jnp.where(low, first, pltpu.roll(second, width, 1))
        out[other] = jnp.where(low, pltpu.roll(first, LANES - width, 1), second)
    return out


def place():
    qa = lax.axis_index("qa")
    qb = lax.axis_index("qb")
    return qa // 2, qa % 2, qb // 4, qb % 4


def kernel_a(
    amps_hbm, mats_hbm, order_hbm, pairs_hbm, angles_hbm, out_hbm,
    amps, mats, order, pairs, angles, out, sems, out_sems,
):
    sources = (mats_hbm.at[1], order_hbm, pairs_hbm, angles_hbm, amps_hbm)
    targets = (mats, order, pairs, angles, amps)
    copies = [
        pltpu.make_async_copy(source, target, sems.at[number])
        for number, (source, target) in enumerate(zip(sources, targets))
    ]
    for copy in copies:
        copy.start()
    for copy in copies[:4]:
        copy.wait()
    block = full_block(gate_block(mats, order, 1))
    yz, core, zh, x = place()
    device = yz * (1 << 20) + core * (1 << 19) + zh * (1 << 18) + x * (1 << 16)
    phase = Phase(pairs, angles, 0, iota(0) * 512 + iota(1))
    copies[4].wait()
    written = []
    for mid in range(4):
        real = amps[pl.ds(2 * mid, 128, stride=8), :]
        imag = amps[pl.ds(2 * mid + 1, 128, stride=8), :]
        real, imag = rotate(phase.factor(device + mid * 128), real, imag)
        values = jnp.concatenate([real, imag], axis=1)
        result = product(mul_t, block, values)
        for part in range(2):
            tiles = result[part * 128 : (part + 1) * 128].reshape(16, 8, LANES)
            out[mid * 16 : (mid + 1) * 16, part * 8 : (part + 1) * 8, :] = tiles
        piece = pl.ds(mid * 16, 16)
        written.append(pltpu.make_async_copy(out.at[piece], out_hbm.at[piece], out_sems.at[mid]))
        written[-1].start()
    for copy in written:
        copy.wait()


def kernel_tables(mats_ref, order_ref, pairs_ref, angles_ref, gates_ref, factors_ref):
    yz, core, zh, x = place()
    row, lane = iota(0), iota(1)
    index = (row // 32) * (1 << 14) + (row % 32) * (1 << 19) + (lane // 32) + (lane % 32) * 512
    phase = Phase(pairs_ref, angles_ref, 1, index)
    device = yz * (1 << 4) + core * (1 << 3) + zh * (1 << 8) + x * (1 << 16)
    for u in range(4):
        factor = phase.factor(device + (u // 2) * (1 << 18) + (u % 2) * 4)
        for part in range(2):
            factors_ref[0, part, u] = factor[part]
    index = (row // 16) * (1 << 16) + (row % 16) + (lane // 32) * (1 << 14) + (lane % 32) * (1 << 19)
    phase = Phase(pairs_ref, angles_ref, 2, index)
    device = yz * (1 << 4) + core * (1 << 11) + zh * (1 << 8) + x * (1 << 12)
    for xl in range(4):
        factor = phase.factor(device + xl * 512)
        for part in range(2):
            factors_ref[1, part, xl] = factor[part]
    natural = iota(0)
    arrived = take_bits(natural, (0, 1, 2, 6, 3, 4, 5))
    for slot, gate in enumerate((0, 3, 2, 4, 5)):
        rows = natural
        columns = arrived if gate == 2 else natural
        blocks = gate_block(
            mats_ref.at[gate], order_ref, gate, rows, None if rows is columns else columns
        )
        if gate == 3:
            for half, (vr, vi) in enumerate(blocks):
                vr, vi = vr.astype(F32), vi.astype(F32)
                top = jnp.concatenate([vr, -vi], axis=1).reshape(32, 4, 256)
                bottom = jnp.concatenate([vi, vr], axis=1).reshape(32, 4, 256)
                mixed = jnp.concatenate([top, bottom], axis=1).reshape(256, 256)
                gates_ref[slot, half] = mixed.astype(BF16)
        else:
            for half, block in enumerate(full_block(blocks)):
                gates_ref[slot, half] = block


def kernel_b(amps_ref, gates_ref, factors_ref, out_ref):
    block_0 = (gates_ref[0, 0], gates_ref[0, 1])
    block_3 = (gates_ref[1, 0], gates_ref[1, 1])
    columns = []
    for u in range(4):
        parts = []
        for part in range(2):
            start = (u // 2) * 512 + part * 8 + (u % 2) * 4
            tiles = [amps_ref[pl.ds(start + t, 32, stride=16), :] for t in range(4)]
            tiles = swap_bit(swap_bit(tiles, 1, 6), 0, 5)
            parts += tiles
        columns.append(jnp.concatenate(parts, axis=0))
    result = product(mul, block_0, jnp.concatenate(columns, axis=1))
    rows = []
    for u in range(4):
        real = result[:128, u * 128 : (u + 1) * 128]
        imag = result[128:, u * 128 : (u + 1) * 128]
        parts = []
        for value in rotate((factors_ref[0, 0, u], factors_ref[0, 1, u]), real, imag):
            tiles = [value[ah * 32 : (ah + 1) * 32] for ah in range(4)]
            tiles = swap_bit(swap_bit(tiles, 1, 6), 0, 5)
            parts.append(jnp.concatenate(tiles, axis=0))
        rows.append(jnp.concatenate(parts, axis=1))
    result = product(mul_t, block_3, jnp.concatenate(rows, axis=0))
    for u in range(4):
        values = result[:, u * 128 : (u + 1) * 128]
        tiles = [values[ah * 64 : (ah + 1) * 64] for ah in range(4)]
        tiles = swap_bit(swap_bit(tiles, 1, 6), 0, 5)
        for t in range(4):
            out_ref[:, u * 4 + t, :, :] = tiles[t].reshape(8, 8, LANES)


def kernel_c(amps_ref, gates_ref, factors_ref, out_ref):
    block_2 = (gates_ref[2, 0], gates_ref[2, 1])
    block_4 = (gates_ref[3, 0], gates_ref[3, 1])
    columns = []
    for xl in range(4):
        parts = [amps_ref[pl.ds(part * 4 + xl, 128, stride=8), :] for part in range(2)]
        columns.append(jnp.concatenate(parts, axis=0))
    result = product(mul, block_2, jnp.concatenate(columns, axis=1))
    rotated = [
        rotate(
            (factors_ref[1, 0, xl], factors_ref[1, 1, xl]),
            result[:128, xl * 128 : (xl + 1) * 128],
            result[128:, xl * 128 : (xl + 1) * 128],
        )
        for xl in range(4)
    ]
    rows = []
    for gb in range(8):
        for xl in range(4):
            real, imag = rotated[xl]
            rows.append(
                jnp.concatenate(
                    [real[gb * 16 : (gb + 1) * 16], imag[gb * 16 : (gb + 1) * 16]], axis=1
                )
            )
    result = product(mul_t, block_4, jnp.concatenate(rows, axis=0))
    for pair in range(4):
        values = result[:, pair * 128 : (pair + 1) * 128]
        tiles = swap_bit([values[:128], values[128:]], 0, 6)
        for last in range(2):
            gb = pair * 2 + last
            for ah in range(4):
                out_ref[pl.ds(gb * 4 + ah, 32, stride=32), :] = tiles[last][ah * 32 : (ah + 1) * 32]


def kernel_d(amps_ref, gates_ref, out_hbm, out, sems):
    block = (gates_ref[4, 0], gates_ref[4, 1])
    written = []
    for b13 in range(2):
        rows = []
        for b7 in range(2):
            tiles = []
            for xb in range(8):
                start = b7 * 512 + xb * 64 + b13 * 8
                tiles.append(
                    jnp.concatenate(
                        [amps_ref[start + 16 * at : start + 16 * at + 8, :] for at in range(4)], axis=0
                    )
                )
            tiles = swap_bit(swap_bit(swap_bit(tiles, 2, 6), 1, 5), 0, 4)
            for xl in range(4):
                rows.append(jnp.concatenate([tiles[xl], tiles[4 + xl]], axis=1))
        result = product(mul_t, block, jnp.concatenate(rows, axis=0), values_left=True)
        for b7, xl, b11, b8, b12 in itertools.product(range(2), range(4), *[range(2)] * 3):
            at = (b7 * 4 + xl) * 32 + b11 * 16 + b8 * 8 + b12 * 4
            to = b13 * 64 + b12 * 32 + b11 * 16 + xl * 4 + b8 * 2 + b7
            for part in range(2):
                out[pl.ds(2 * to + part, 4, stride=256), :] = result[
                    at : at + 4, part * 128 : (part + 1) * 128
                ]
        for ah in range(4):
            piece = pl.ds(ah * 256 + b13 * 128, 128)
            written.append(
                pltpu.make_async_copy(out.at[piece], out_hbm.at[piece], sems.at[b13 * 4 + ah])
            )
            written[-1].start()
    for copy in written:
        copy.wait()


VMEM = pl.BlockSpec(memory_space=pltpu.VMEM)
HBM = pl.BlockSpec(memory_space=pltpu.HBM)
TABLES = (
    jax.ShapeDtypeStruct((5, 2, 256, 256), BF16),
    jax.ShapeDtypeStruct((2, 2, 4, 128, LANES), F32),
)


def call(kernel, name, out_shape, *operands, space=VMEM, out_space=VMEM, scratch=(), mib=24):
    return pl.pallas_call(
        kernel,
        out_shape=out_shape,
        in_specs=[space] * len(operands),
        out_specs=jax.tree.map(lambda _: out_space, out_shape),
        scratch_shapes=list(scratch),
        compiler_params=pltpu.CompilerParams(vmem_limit_bytes=mib * 1024 * 1024),
        cost_estimate=pl.CostEstimate(flops=400_000_000, bytes_accessed=2_000_000, transcendentals=0),
        name=name,
    )(*operands)


def body(amplitudes, gate_mats, gate_order, phase_pairs, phase_angles):
    pairs = phase_pairs.transpose(0, 2, 1)
    shared = (gate_mats, gate_order, pairs, phase_angles)
    shape = jax.ShapeDtypeStruct((1024, LANES), F32)
    state = amplitudes.reshape(2, 512, LANES).transpose(1, 0, 2).reshape(1024, LANES)
    state = call(
        kernel_a,
        "first_gate",
        jax.ShapeDtypeStruct((64, 16, LANES), F32),
        state,
        *shared,
        space=HBM,
        out_space=HBM,
        mib=63,
        scratch=(
            pltpu.VMEM((1024, LANES), F32),
            pltpu.VMEM((2, 128, LANES), F32),
            pltpu.VMEM((6, 7), jnp.int32),
            pltpu.VMEM((3, 2, 4), jnp.int32),
            pltpu.VMEM((3, 4), F32),
            pltpu.VMEM((64, 16, LANES), F32),
            pltpu.SemaphoreType.DMA((5,)),
            pltpu.SemaphoreType.DMA((4,)),
        ),
    )
    state = exchange(state, ["zh", "y", "zl", "c"]).reshape(1024, LANES)
    gates, factors = call(kernel_tables, "tables", TABLES, *shared)
    state = call(
        kernel_b, "second_gates", jax.ShapeDtypeStruct((8, 16, 8, LANES), F32), state, gates, factors
    )
    state = exchange(state.reshape(1024, LANES), ["x", "c"])
    state = call(kernel_c, "third_gates", shape, state, gates, factors)
    state = exchange(state, ["y", "zl", "c", "zh", "x"])
    state = call(
        kernel_d,
        "last_gate",
        shape,
        state,
        gates,
        out_space=HBM,
        scratch=(pltpu.VMEM((1024, LANES), F32), pltpu.SemaphoreType.DMA((8,))),
    )
    return state.reshape(512, 2, LANES).transpose(1, 0, 2).reshape(2, 65536)


def solution(mesh):
    return jax.shard_map(
        body,
        mesh=mesh,
        in_specs=(P(None, AXES), P(), P(), P(), P()),
        out_specs=P(None, AXES),
        check_vma=False,
    )
```

```python
import itertools

import jax
import jax.numpy as jnp
from jax import lax
from jax.experimental import pallas as pl
from jax.experimental.pallas import tpu as pltpu
from jax.sharding import PartitionSpec as P

AXES = ("qa", "qb")
SIZES = {"y": 4, "zl": 4, "c": 2, "zh": 2, "x": 4}
F32 = jnp.float32
BF16 = jnp.bfloat16
LANES = 128


def device_groups(varying):
    fixed = [name for name in SIZES if name not in varying]
    groups = []
    for held in itertools.product(*[range(SIZES[name]) for name in fixed]):
        group = []
        for moved in itertools.product(*[range(SIZES[name]) for name in varying]):
            at = dict(zip(fixed, held)) | dict(zip(varying, moved))
            group.append((at["y"] * 8 + at["zl"] * 2 + at["c"]) * 8 + at["zh"] * 4 + at["x"])
        groups.append(group)
    return groups


def exchange(values, varying):
    groups = device_groups(varying)
    parts = values.reshape(len(groups[0]), -1, LANES)
    if len(groups) == 1:
        moved = lax.all_to_all(parts, AXES, 0, 0, tiled=True)
    else:
        moved = lax.all_to_all(parts, AXES, 0, 0, axis_index_groups=groups, tiled=True)
    return moved.reshape(values.shape)


def from_partner(value, varying, mask):
    pairs = [
        (group[at], group[at ^ mask]) for group in device_groups([varying]) for at in range(len(group))
    ]
    return lax.ppermute(value, AXES, pairs)


def iota(axis, shape=(128, 128)):
    return lax.broadcasted_iota(jnp.int32, shape, axis)


def take_bits(index, places):
    total = None
    for source, place in enumerate(places):
        bit = jnp.left_shift(jnp.bitwise_and(jnp.right_shift(index, source), 1), place)
        total = bit if total is None else total + bit
    return total


def onehot(order_ref, gate, index):
    mapped = None
    order = order_ref[...]
    for target in range(7):
        shift = order[gate : gate + 1, target : target + 1]
        bit = jnp.bitwise_and(jnp.right_shift(index, shift), 1)
        bit = jnp.left_shift(bit, target)
        mapped = bit if mapped is None else mapped + bit
    return (mapped == iota(1)).astype(F32).astype(BF16)


def mul(left, right):
    return jnp.dot(left, right, preferred_element_type=F32)


def mul_t(left, right):
    return lax.dot_general(left, right, (((1,), (1,)), ((), ())), preferred_element_type=F32)


def halves(values):
    high = values.astype(BF16)
    return high, (values - high.astype(F32)).astype(BF16)


def gate_block(mats, order_ref, gate, rows=None, columns=None):
    rows = onehot(order_ref, gate, iota(0) if rows is None else rows)
    columns = rows if columns is None else onehot(order_ref, gate, columns)
    parts = [half for part in range(2) for half in halves(mats[part])]
    turned = mul_t(columns, jnp.concatenate(parts, axis=0)).astype(BF16)
    parts = [mul_t(rows, turned[:, at * 128 : (at + 1) * 128]).astype(BF16) for at in range(4)]
    return [(parts[0], parts[2]), (parts[1], parts[3])]


def full_block(blocks):
    out = []
    for vr, vi in blocks:
        out.append(
            jnp.concatenate(
                [jnp.concatenate([vr, -vi], axis=1), jnp.concatenate([vi, vr], axis=1)], axis=0
            )
        )
    return out


def product(multiply, block, values, values_left=False):
    high, low = halves(values)
    block_high, block_low = block
    if values_left:
        return multiply(high, block_high) + (multiply(low, block_high) + multiply(high, block_low))
    return multiply(block_high, high) + (multiply(block_high, low) + multiply(block_low, high))


def sign_of(index, pairs, layer, term):
    first = jnp.right_shift(index, pairs[layer, 0:1, term : term + 1])
    second = jnp.right_shift(index, pairs[layer, 1:2, term : term + 1])
    bit = jnp.bitwise_and(jnp.bitwise_xor(first, second), 1)
    return (1 - 2 * bit).astype(F32)


class Phase:
    def __init__(self, pairs_ref, angles_ref, layer, index):
        self.pairs = pairs_ref[...]
        self.layer = layer
        angles = angles_ref[...]
        cosine = jnp.cos(angles)
        sine = jnp.sin(angles)
        self.cosine = [cosine[layer : layer + 1, term : term + 1] for term in range(4)]
        self.sine = [
            sine[layer : layer + 1, term : term + 1] * sign_of(index, self.pairs, layer, term)
            for term in range(4)
        ]

    def factor(self, rest):
        rest = jnp.full((1, 1), rest, jnp.int32)
        factors = []
        for term in range(4):
            sign = sign_of(rest, self.pairs, self.layer, term)
            factors.append((self.cosine[term], self.sine[term] * sign))

        def pair(first, second):
            return (
                first[0] * second[0] - first[1] * second[1],
                first[0] * second[1] + first[1] * second[0],
            )

        return pair(pair(factors[0], factors[1]), pair(factors[2], factors[3]))


def rotate(factor, real, imag):
    cosine, sine = factor
    return real * cosine - imag * sine, real * sine + imag * cosine


def swap_bit(tiles, tile_bit, lane_bit):
    width = 1 << lane_bit
    lane = iota(1, tiles[0].shape)
    low = jnp.bitwise_and(lane, width) == 0
    out = list(tiles)
    for number in range(len(tiles)):
        other = number | (1 << tile_bit)
        if other == number:
            continue
        first, second = tiles[number], tiles[other]
        if 2 * width == LANES:
            moved = pltpu.roll(jnp.where(low, second, first), width, 1)
            out[number] = jnp.where(low, first, moved)
            out[other] = jnp.where(low, moved, second)
            continue
        out[number] = jnp.where(low, first, pltpu.roll(second, width, 1))
        out[other] = jnp.where(low, pltpu.roll(first, LANES - width, 1), second)
    return out


def place():
    qa = lax.axis_index("qa")
    qb = lax.axis_index("qb")
    return qa // 2, qa % 2, qb // 4, qb % 4


def kernel_a(
    amps_hbm, mats_hbm, order_hbm, pairs_hbm, angles_hbm, out_hbm,
    amps, mats, order, pairs, angles, out, sems, out_sems,
):
    sources = (mats_hbm.at[1], order_hbm, pairs_hbm, angles_hbm, amps_hbm)
    targets = (mats, order, pairs, angles, amps)
    copies = [
        pltpu.make_async_copy(source, target, sems.at[number])
        for number, (source, target) in enumerate(zip(sources, targets))
    ]
    for copy in copies:
        copy.start()
    for copy in copies[:4]:
        copy.wait()
    block = full_block(gate_block(mats, order, 1))
    yz, core, zh, x = place()
    device = yz * (1 << 20) + core * (1 << 19) + zh * (1 << 18) + x * (1 << 16)
    phase = Phase(pairs, angles, 0, iota(0) * 512 + iota(1))
    copies[4].wait()
    written = []
    for mid in range(4):
        real = amps[pl.ds(2 * mid, 128, stride=8), :]
        imag = amps[pl.ds(2 * mid + 1, 128, stride=8), :]
        real, imag = rotate(phase.factor(device + mid * 128), real, imag)
        values = jnp.concatenate([real, imag], axis=1)
        result = product(mul_t, block, values)
        for part in range(2):
            tiles = result[part * 128 : (part + 1) * 128].reshape(16, 8, LANES)
            out[mid * 16 : (mid + 1) * 16, part * 8 : (part + 1) * 8, :] = tiles
        piece = pl.ds(mid * 16, 16)
        written.append(pltpu.make_async_copy(out.at[piece], out_hbm.at[piece], out_sems.at[mid]))
        written[-1].start()
    for copy in written:
        copy.wait()


def kernel_tables(mats_ref, order_ref, pairs_ref, angles_ref, gates_ref, factors_ref):
    yz, core, zh, x = place()
    row, lane = iota(0), iota(1)
    index = (row // 32) * (1 << 14) + (row % 32) * (1 << 19) + (lane // 32) + (lane % 32) * 512
    phase = Phase(pairs_ref, angles_ref, 1, index)
    device = yz * (1 << 4) + core * (1 << 3) + zh * (1 << 8) + x * (1 << 16)
    for u in range(4):
        factor = phase.factor(device + (u // 2) * (1 << 18) + (u % 2) * 4)
        for part in range(2):
            factors_ref[0, part, u] = factor[part]
    index = (row // 16) * (1 << 16) + (row % 16) + (lane // 32) * (1 << 14) + (lane % 32) * (1 << 19)
    phase = Phase(pairs_ref, angles_ref, 2, index)
    device = yz * (1 << 4) + core * (1 << 11) + zh * (1 << 8) + x * (1 << 12)
    for xl in range(4):
        factor = phase.factor(device + xl * 512)
        for part in range(2):
            factors_ref[1, part, xl] = factor[part]
    natural = iota(0)
    arrived = take_bits(natural, (0, 1, 2, 6, 3, 4, 5))
    for slot, gate in enumerate((0, 3, 2, 4, 5)):
        rows = natural ^ (x * 8 + core * 4) if gate == 3 else natural
        columns = arrived ^ (x * 16 + core * 8) if gate == 2 else natural
        blocks = gate_block(
            mats_ref.at[gate], order_ref, gate, rows, None if rows is columns else columns
        )
        if gate == 3:
            for half, (vr, vi) in enumerate(blocks):
                vr, vi = vr.astype(F32), vi.astype(F32)
                top = jnp.concatenate([vr, -vi], axis=1).reshape(32, 4, 256)
                bottom = jnp.concatenate([vi, vr], axis=1).reshape(32, 4, 256)
                mixed = jnp.concatenate([top, bottom], axis=1).reshape(256, 256)
                gates_ref[slot, half] = mixed.astype(BF16)
        else:
            for half, block in enumerate(full_block(blocks)):
                gates_ref[slot, half] = block


def kernel_b(amps_ref, gates_ref, factors_ref, kept_ref, sent_ref):
    block_0 = (gates_ref[0, 0], gates_ref[0, 1])
    block_3 = (gates_ref[1, 0], gates_ref[1, 1])
    columns = []
    for u in range(4):
        parts = []
        for part in range(2):
            start = (u // 2) * 512 + part * 8 + (u % 2) * 4
            tiles = [amps_ref[pl.ds(start + t, 32, stride=16), :] for t in range(4)]
            tiles = swap_bit(swap_bit(tiles, 1, 6), 0, 5)
            parts += tiles
        columns.append(jnp.concatenate(parts, axis=0))
    result = product(mul, block_0, jnp.concatenate(columns, axis=1))
    rows = []
    for u in range(4):
        real = result[:128, u * 128 : (u + 1) * 128]
        imag = result[128:, u * 128 : (u + 1) * 128]
        parts = []
        for value in rotate((factors_ref[0, 0, u], factors_ref[0, 1, u]), real, imag):
            tiles = [value[ah * 32 : (ah + 1) * 32] for ah in range(4)]
            tiles = swap_bit(swap_bit(tiles, 1, 6), 0, 5)
            parts.append(jnp.concatenate(tiles, axis=0))
        rows.append(jnp.concatenate(parts, axis=1))
    result = product(mul_t, block_3, jnp.concatenate(rows, axis=0))
    for u in range(4):
        values = result[:, u * 128 : (u + 1) * 128]
        tiles = [values[ah * 64 : (ah + 1) * 64] for ah in range(4)]
        tiles = swap_bit(swap_bit(tiles, 1, 6), 0, 5)
        for t in range(4):
            to = (u * 4 + t) * 8
            for k in range(4):
                kept_ref[k, to : to + 8, :] = tiles[t][k * 16 : k * 16 + 8]
                sent_ref[k, to : to + 8, :] = tiles[t][k * 16 + 8 : k * 16 + 16]


def kernel_c(kept_ref, got_ref, *refs):
    arrived, (gates_ref, factors_ref, out_ref) = refs[:3], refs[3:]
    block_2 = (gates_ref[2, 0], gates_ref[2, 1])
    block_4 = (gates_ref[3, 0], gates_ref[3, 1])
    columns = []
    for xl in range(4):
        parts = []
        for part in range(2):
            rows = pl.ds(part * 4 + xl, 16, stride=8)
            parts += [kept_ref[0, rows, :], got_ref[0, rows, :]]
            for ref in (arrived[2], arrived[0], arrived[1]):
                parts += [ref[0, rows, :], ref[1, rows, :]]
        columns.append(jnp.concatenate(parts, axis=0))
    result = product(mul, block_2, jnp.concatenate(columns, axis=1))
    rotated = [
        rotate(
            (factors_ref[1, 0, xl], factors_ref[1, 1, xl]),
            result[:128, xl * 128 : (xl + 1) * 128],
            result[128:, xl * 128 : (xl + 1) * 128],
        )
        for xl in range(4)
    ]
    rows = []
    for gb in range(8):
        for xl in range(4):
            real, imag = rotated[xl]
            rows.append(
                jnp.concatenate(
                    [real[gb * 16 : (gb + 1) * 16], imag[gb * 16 : (gb + 1) * 16]], axis=1
                )
            )
    result = product(mul_t, block_4, jnp.concatenate(rows, axis=0))
    for pair in range(4):
        values = result[:, pair * 128 : (pair + 1) * 128]
        tiles = swap_bit([values[:128], values[128:]], 0, 6)
        for last in range(2):
            gb = pair * 2 + last
            for ah in range(4):
                out_ref[pl.ds(gb * 4 + ah, 32, stride=32), :] = tiles[last][ah * 32 : (ah + 1) * 32]


def kernel_d(amps_ref, gates_ref, out_hbm, out, sems):
    block = (gates_ref[4, 0], gates_ref[4, 1])
    written = []
    for b13 in range(2):
        rows = []
        for b7 in range(2):
            tiles = []
            for xb in range(8):
                start = b7 * 512 + xb * 64 + b13 * 8
                tiles.append(
                    jnp.concatenate(
                        [amps_ref[start + 16 * at : start + 16 * at + 8, :] for at in range(4)], axis=0
                    )
                )
            tiles = swap_bit(swap_bit(swap_bit(tiles, 2, 6), 1, 5), 0, 4)
            for xl in range(4):
                rows.append(jnp.concatenate([tiles[xl], tiles[4 + xl]], axis=1))
        result = product(mul_t, block, jnp.concatenate(rows, axis=0), values_left=True)
        for b7, xl, b11, b8, b12 in itertools.product(range(2), range(4), *[range(2)] * 3):
            at = (b7 * 4 + xl) * 32 + b11 * 16 + b8 * 8 + b12 * 4
            to = b13 * 64 + b12 * 32 + b11 * 16 + xl * 4 + b8 * 2 + b7
            for part in range(2):
                out[pl.ds(2 * to + part, 4, stride=256), :] = result[
                    at : at + 4, part * 128 : (part + 1) * 128
                ]
        for ah in range(4):
            piece = pl.ds(ah * 256 + b13 * 128, 128)
            written.append(
                pltpu.make_async_copy(out.at[piece], out_hbm.at[piece], sems.at[b13 * 4 + ah])
            )
            written[-1].start()
    for copy in written:
        copy.wait()


VMEM = pl.BlockSpec(memory_space=pltpu.VMEM)
HBM = pl.BlockSpec(memory_space=pltpu.HBM)
TABLES = (
    jax.ShapeDtypeStruct((5, 2, 256, 256), BF16),
    jax.ShapeDtypeStruct((2, 2, 4, 128, LANES), F32),
)


def call(kernel, name, out_shape, *operands, space=VMEM, out_space=VMEM, scratch=(), mib=24):
    return pl.pallas_call(
        kernel,
        out_shape=out_shape,
        in_specs=[space] * len(operands),
        out_specs=jax.tree.map(lambda _: out_space, out_shape),
        scratch_shapes=list(scratch),
        compiler_params=pltpu.CompilerParams(vmem_limit_bytes=mib * 1024 * 1024),
        cost_estimate=pl.CostEstimate(flops=400_000_000, bytes_accessed=2_000_000, transcendentals=0),
        name=name,
    )(*operands)


def body(amplitudes, gate_mats, gate_order, phase_pairs, phase_angles):
    pairs = phase_pairs.transpose(0, 2, 1)
    shared = (gate_mats, gate_order, pairs, phase_angles)
    shape = jax.ShapeDtypeStruct((1024, LANES), F32)
    state = amplitudes.reshape(2, 512, LANES).transpose(1, 0, 2).reshape(1024, LANES)
    state = call(
        kernel_a,
        "first_gate",
        jax.ShapeDtypeStruct((64, 16, LANES), F32),
        state,
        *shared,
        space=HBM,
        out_space=HBM,
        mib=63,
        scratch=(
            pltpu.VMEM((1024, LANES), F32),
            pltpu.VMEM((2, 128, LANES), F32),
            pltpu.VMEM((6, 7), jnp.int32),
            pltpu.VMEM((3, 2, 4), jnp.int32),
            pltpu.VMEM((3, 4), F32),
            pltpu.VMEM((64, 16, LANES), F32),
            pltpu.SemaphoreType.DMA((5,)),
            pltpu.SemaphoreType.DMA((4,)),
        ),
    )
    state = exchange(state, ["zh", "y", "zl", "c"]).reshape(1024, LANES)
    gates, factors = call(kernel_tables, "tables", TABLES, *shared)
    half = jax.ShapeDtypeStruct((4, 128, LANES), F32)
    kept, sent = call(kernel_b, "second_gates", (half, half), state, gates, factors)
    got = from_partner(sent, "c", 1)
    arrived = {k: from_partner(jnp.stack([kept[k], got[k]]), "x", k) for k in (2, 3, 1)}
    state = call(
        kernel_c, "third_gates", shape, kept, got, arrived[2], arrived[3], arrived[1], gates, factors
    )
    state = exchange(state, ["y", "zl", "c", "zh", "x"])
    state = call(
        kernel_d,
        "last_gate",
        shape,
        state,
        gates,
        out_space=HBM,
        scratch=(pltpu.VMEM((1024, LANES), F32), pltpu.SemaphoreType.DMA((8,))),
    )
    return state.reshape(512, 2, LANES).transpose(1, 0, 2).reshape(2, 65536)


def solution(mesh):
    return jax.shard_map(
        body,
        mesh=mesh,
        in_specs=(P(None, AXES), P(), P(), P(), P()),
        out_specs=P(None, AXES),
        check_vma=False,
    )
```

```python
import itertools

import jax
import jax.numpy as jnp
from jax import lax
from jax.experimental import pallas as pl
from jax.experimental.pallas import tpu as pltpu
from jax.sharding import PartitionSpec as P

AXES = ("qa", "qb")
SIZES = {"y": 4, "zl": 4, "c": 2, "zh": 2, "x": 4}
F32 = jnp.float32
BF16 = jnp.bfloat16
LANES = 128


def device_groups(varying):
    fixed = [name for name in SIZES if name not in varying]
    groups = []
    for held in itertools.product(*[range(SIZES[name]) for name in fixed]):
        group = []
        for moved in itertools.product(*[range(SIZES[name]) for name in varying]):
            at = dict(zip(fixed, held)) | dict(zip(varying, moved))
            group.append((at["y"] * 8 + at["zl"] * 2 + at["c"]) * 8 + at["zh"] * 4 + at["x"])
        groups.append(group)
    return groups


def exchange(values, varying):
    groups = device_groups(varying)
    parts = values.reshape(len(groups[0]), -1, LANES)
    moved = lax.all_to_all(parts, AXES, 0, 0, axis_index_groups=groups, tiled=True)
    return moved.reshape(values.shape)


def from_partner(value, varying, mask):
    pairs = [
        (group[at], group[at ^ mask]) for group in device_groups([varying]) for at in range(len(group))
    ]
    return lax.ppermute(value, AXES, pairs)


def iota(axis, shape=(128, 128)):
    return lax.broadcasted_iota(jnp.int32, shape, axis)


def take_bits(index, places):
    total = None
    for source, place in enumerate(places):
        bit = jnp.left_shift(jnp.bitwise_and(jnp.right_shift(index, source), 1), place)
        total = bit if total is None else total + bit
    return total


def onehot(order_ref, gate, index):
    mapped = None
    order = order_ref[...]
    for target in range(7):
        shift = order[gate : gate + 1, target : target + 1]
        bit = jnp.bitwise_and(jnp.right_shift(index, shift), 1)
        bit = jnp.left_shift(bit, target)
        mapped = bit if mapped is None else mapped + bit
    return (mapped == iota(1)).astype(F32).astype(BF16)


def mul(left, right):
    return jnp.dot(left, right, preferred_element_type=F32)


def mul_t(left, right):
    return lax.dot_general(left, right, (((1,), (1,)), ((), ())), preferred_element_type=F32)


def halves(values):
    high = values.astype(BF16)
    return high, (values - high.astype(F32)).astype(BF16)


def gate_block(mats, order_ref, gate, rows=None, columns=None):
    rows = onehot(order_ref, gate, iota(0) if rows is None else rows)
    columns = rows if columns is None else onehot(order_ref, gate, columns)
    parts = [half for part in range(2) for half in halves(mats[part])]
    turned = mul_t(columns, jnp.concatenate(parts, axis=0)).astype(BF16)
    parts = [mul_t(rows, turned[:, at * 128 : (at + 1) * 128]).astype(BF16) for at in range(4)]
    return [(parts[0], parts[2]), (parts[1], parts[3])]


def full_block(blocks):
    out = []
    for vr, vi in blocks:
        out.append(
            jnp.concatenate(
                [jnp.concatenate([vr, -vi], axis=1), jnp.concatenate([vi, vr], axis=1)], axis=0
            )
        )
    return out


def thrice(high, low):
    return jnp.concatenate([high, high, low], axis=1)


def product(multiply, block, values, values_left=False):
    high, low = halves(values)
    values = jnp.concatenate([high, low, high], axis=0 if multiply is mul else 1)
    return multiply(values, block) if values_left else multiply(block, values)


def sign_of(index, pairs, layer, term):
    first = jnp.right_shift(index, pairs[layer, 0:1, term : term + 1])
    second = jnp.right_shift(index, pairs[layer, 1:2, term : term + 1])
    bit = jnp.bitwise_and(jnp.bitwise_xor(first, second), 1)
    return (1 - 2 * bit).astype(F32)


class Phase:
    def __init__(self, pairs_ref, angles_ref, layer, index):
        self.pairs = pairs_ref[...]
        self.layer = layer
        angles = angles_ref[...]
        cosine = jnp.cos(angles)
        sine = jnp.sin(angles)
        self.cosine = [cosine[layer : layer + 1, term : term + 1] for term in range(4)]
        self.sine = [
            sine[layer : layer + 1, term : term + 1] * sign_of(index, self.pairs, layer, term)
            for term in range(4)
        ]

    def factor(self, rest):
        rest = jnp.full((1, 1), rest, jnp.int32)
        factors = []
        for term in range(4):
            sign = sign_of(rest, self.pairs, self.layer, term)
            factors.append((self.cosine[term], self.sine[term] * sign))

        def pair(first, second):
            return (
                first[0] * second[0] - first[1] * second[1],
                first[0] * second[1] + first[1] * second[0],
            )

        return pair(pair(factors[0], factors[1]), pair(factors[2], factors[3]))


def rotate(factor, real, imag):
    cosine, sine = factor
    return real * cosine - imag * sine, real * sine + imag * cosine


def swap_bit(tiles, tile_bit, lane_bit):
    width = 1 << lane_bit
    lane = iota(1, tiles[0].shape)
    low = jnp.bitwise_and(lane, width) == 0
    out = list(tiles)
    for number in range(len(tiles)):
        other = number | (1 << tile_bit)
        if other == number:
            continue
        first, second = tiles[number], tiles[other]
        if 2 * width == LANES:
            moved = pltpu.roll(jnp.where(low, second, first), width, 1)
            out[number] = jnp.where(low, first, moved)
            out[other] = jnp.where(low, moved, second)
            continue
        out[number] = jnp.where(low, first, pltpu.roll(second, width, 1))
        out[other] = jnp.where(low, pltpu.roll(first, LANES - width, 1), second)
    return out


def place():
    qa = lax.axis_index("qa")
    qb = lax.axis_index("qb")
    return qa // 8, qa // 2 % 4, qa % 2, qb // 4, qb % 4


def kernel_a(
    amps_hbm, mats_hbm, order_hbm, pairs_hbm, angles_hbm, out_hbm,
    amps, mats, order, pairs, angles, out, sems, out_sems,
):
    sources = (mats_hbm.at[1], order_hbm, pairs_hbm, angles_hbm, amps_hbm)
    targets = (mats, order, pairs, angles, amps)
    copies = [
        pltpu.make_async_copy(source, target, sems.at[number])
        for number, (source, target) in enumerate(zip(sources, targets))
    ]
    for copy in copies:
        copy.start()
    for copy in copies[:4]:
        copy.wait()
    block = thrice(*full_block(gate_block(mats, order, 1)))
    y, zl, core, zh, x = place()
    device = y * (1 << 22) + zl * (1 << 20) + core * (1 << 19) + zh * (1 << 18) + x * (1 << 16)
    phase = Phase(pairs, angles, 0, iota(0) * 512 + iota(1))
    copies[4].wait()
    written = []
    for mid in range(4):
        real = amps[pl.ds(2 * mid, 128, stride=8), :]
        imag = amps[pl.ds(2 * mid + 1, 128, stride=8), :]
        real, imag = rotate(phase.factor(device + mid * 128), real, imag)
        values = jnp.concatenate([real, imag], axis=1)
        result = product(mul_t, block, values)
        for part in range(2):
            tiles = result[part * 128 : (part + 1) * 128].reshape(16, 8, LANES)
            out[mid * 16 : (mid + 1) * 16, part * 8 : (part + 1) * 8, :] = tiles
        piece = pl.ds(mid * 16, 16)
        written.append(pltpu.make_async_copy(out.at[piece], out_hbm.at[piece], out_sems.at[mid]))
        written[-1].start()
    for copy in written:
        copy.wait()


def kernel_tables(mats_ref, order_ref, pairs_ref, angles_ref, gates_ref, factors_ref):
    y, zl, core, zh, x = place()
    held = y * (1 << 7) + zh * (1 << 6) + zl * (1 << 4)
    row, lane = iota(0), iota(1)
    index = (row // 32) * (1 << 14) + (row % 32) * (1 << 19) + (lane // 32) + (lane % 32) * 512
    phase = Phase(pairs_ref, angles_ref, 1, index)
    device = held + core * (1 << 3) + x * (1 << 16)
    for u in range(4):
        factor = phase.factor(device + (u // 2) * (1 << 18) + (u % 2) * 4)
        for part in range(2):
            factors_ref[0, part, u] = factor[part]
    index = (row // 16) * (1 << 16) + (row % 16) + (lane // 32) * (1 << 14) + (lane % 32) * (1 << 19)
    phase = Phase(pairs_ref, angles_ref, 2, index)
    device = held + core * (1 << 13) + x * (1 << 11)
    for xl in range(4):
        factor = phase.factor(device + xl * 512)
        for part in range(2):
            factors_ref[1, part, xl] = factor[part]
    natural = iota(0)
    arrived = take_bits(natural, (0, 1, 2, 6, 3, 4, 5))
    leaving = take_bits(natural, (0, 3, 4, 1, 2, 5, 6))
    for slot, gate in enumerate((0, 3, 2, 4, 5)):
        rows = columns = natural
        if gate == 3:
            rows = natural ^ (core * 16 + x * 4)
        if gate == 2:
            columns = arrived ^ (x * 16 + core * 8)
        if gate == 4:
            rows = leaving
        blocks = gate_block(
            mats_ref.at[gate], order_ref, gate, rows, None if rows is columns else columns
        )
        block = thrice(*full_block(blocks))
        if gate == 3:
            block = block.astype(F32).reshape(2, 32, 4, 768)
            block = jnp.concatenate([block[0], block[1]], axis=1).reshape(256, 768).astype(BF16)
        gates_ref[slot] = block


def kernel_b(amps_ref, gates_ref, factors_ref, kept_ref, soon_ref, later_ref):
    for first in range(0, 4, 2):
        group = range(first, first + 2)
        columns = []
        for u in group:
            parts = []
            for part in range(2):
                start = (u // 2) * 128 + part * 8 + (u % 2) * 4
                tiles = [
                    jnp.concatenate(
                        [amps_ref[pl.ds(y * 256 + start + t, 8, stride=16), :] for y in range(4)], axis=0
                    )
                    for t in range(4)
                ]
                tiles = swap_bit(swap_bit(tiles, 1, 6), 0, 5)
                parts += tiles
            columns.append(jnp.concatenate(parts, axis=0))
        result = product(mul, gates_ref[0], jnp.concatenate(columns, axis=1))
        rows = []
        for at, u in enumerate(group):
            real = result[:128, at * 128 : (at + 1) * 128]
            imag = result[128:, at * 128 : (at + 1) * 128]
            parts = []
            for value in rotate((factors_ref[0, 0, u], factors_ref[0, 1, u]), real, imag):
                tiles = [value[ah * 32 : (ah + 1) * 32] for ah in range(4)]
                tiles = swap_bit(swap_bit(tiles, 1, 6), 0, 5)
                parts.append(jnp.concatenate(tiles, axis=0))
            rows.append(jnp.concatenate(parts, axis=1))
        result = product(mul_t, gates_ref[1], jnp.concatenate(rows, axis=0))
        for at, u in enumerate(group):
            values = result[:, at * 128 : (at + 1) * 128]
            tiles = [values[ah * 64 : (ah + 1) * 64] for ah in range(4)]
            tiles = swap_bit(swap_bit(tiles, 1, 6), 0, 5)
            for t in range(4):
                to = (u * 4 + t) * 8
                for k in range(4):
                    kept_ref[k, to : to + 8, :] = tiles[t][k * 8 : k * 8 + 8]
                    if k == 2:
                        soon_ref[to : to + 8, :] = tiles[t][k * 8 + 32 : k * 8 + 40]
                    else:
                        later_ref[min(k, 2), to : to + 8, :] = tiles[t][k * 8 + 32 : k * 8 + 40]


def kernel_c(kept_ref, got_ref, *refs):
    arrived, (gates_ref, factors_ref, out_ref) = refs[:3], refs[3:]
    rotated = []
    for start in range(0, 4, 2):
        columns = []
        for xl in range(start, start + 2):
            parts = []
            for part in range(2):
                rows = pl.ds(part * 4 + xl, 16, stride=8)
                parts += [kept_ref[0, rows, :], got_ref[0, rows, :]]
                for ref in (arrived[2], arrived[0], arrived[1]):
                    parts += [ref[0, rows, :], ref[1, rows, :]]
            columns.append(jnp.concatenate(parts, axis=0))
        result = product(mul, gates_ref[2], jnp.concatenate(columns, axis=1))
        for at in range(2):
            rotated.append(
                rotate(
                    (factors_ref[1, 0, start + at], factors_ref[1, 1, start + at]),
                    result[:128, at * 128 : (at + 1) * 128],
                    result[128:, at * 128 : (at + 1) * 128],
                )
            )
    for start in range(0, 4, 2):
        rows = []
        for gb in range(2 * start, 2 * (start + 2)):
            for real, imag in rotated:
                at = slice(gb * 16, (gb + 1) * 16)
                rows.append(jnp.concatenate([real[at], imag[at]], axis=1))
        result = product(mul_t, gates_ref[3], jnp.concatenate(rows, axis=0))
        for pair in range(start, start + 2):
            values = result[:, (pair - start) * 128 : (pair - start + 1) * 128]
            tiles = swap_bit([values[:128], values[128:]], 0, 6)
            for last in range(2):
                start_row = (pair // 2) * 512 + (pair % 2 * 2 + last) * 4
                for ah in range(4):
                    rows = pl.ds(start_row + ah, 32, stride=16)
                    out_ref[rows, :] = tiles[last][ah * 32 : (ah + 1) * 32]


def kernel_d(amps_ref, gates_ref, out_hbm, out, sems):
    written = []
    for half in range(2):
        rows = []
        for ah in range(half * 2, half * 2 + 2):
            for mid in range(4):
                tiles = [
                    amps_ref[pl.ds(xb * 128 + mid * 32 + ah, 8, stride=4), :] for xb in range(8)
                ]
                tiles = swap_bit(swap_bit(swap_bit(tiles, 2, 6), 1, 5), 0, 4)
                for xl in range(4):
                    rows.append(jnp.concatenate([tiles[xl], tiles[4 + xl]], axis=1))
        result = product(mul_t, gates_ref[4], jnp.concatenate(rows, axis=0), values_left=True)
        for at, (ah, mid, xl) in enumerate(itertools.product(range(2), range(4), range(4))):
            to = (half * 2 + ah) * 128 + xl * 4 + mid
            for part in range(2):
                out[pl.ds(2 * to + part, 8, stride=32), :] = result[
                    at * 8 : at * 8 + 8, part * 128 : (part + 1) * 128
                ]
        piece = pl.ds(half * 512, 512)
        written.append(pltpu.make_async_copy(out.at[piece], out_hbm.at[piece], sems.at[half]))
        written[-1].start()
    for copy in written:
        copy.wait()


VMEM = pl.BlockSpec(memory_space=pltpu.VMEM)
HBM = pl.BlockSpec(memory_space=pltpu.HBM)
TABLES = (
    jax.ShapeDtypeStruct((5, 256, 768), BF16),
    jax.ShapeDtypeStruct((2, 2, 4, 128, LANES), F32),
)


def call(kernel, name, out_shape, *operands, space=VMEM, out_space=VMEM, scratch=(), mib=24):
    return pl.pallas_call(
        kernel,
        out_shape=out_shape,
        in_specs=[space] * len(operands),
        out_specs=jax.tree.map(lambda _: out_space, out_shape),
        scratch_shapes=list(scratch),
        compiler_params=pltpu.CompilerParams(vmem_limit_bytes=mib * 1024 * 1024),
        cost_estimate=pl.CostEstimate(flops=400_000_000, bytes_accessed=2_000_000, transcendentals=0),
        name=name,
    )(*operands)


def body(amplitudes, gate_mats, gate_order, phase_pairs, phase_angles):
    pairs = phase_pairs.transpose(0, 2, 1)
    shared = (gate_mats, gate_order, pairs, phase_angles)
    shape = jax.ShapeDtypeStruct((1024, LANES), F32)
    state = amplitudes.reshape(2, 512, LANES).transpose(1, 0, 2).reshape(1024, LANES)
    state = call(
        kernel_a,
        "first_gate",
        jax.ShapeDtypeStruct((64, 16, LANES), F32),
        state,
        *shared,
        space=HBM,
        out_space=HBM,
        mib=63,
        scratch=(
            pltpu.VMEM((1024, LANES), F32),
            pltpu.VMEM((2, 128, LANES), F32),
            pltpu.VMEM((6, 7), jnp.int32),
            pltpu.VMEM((3, 2, 4), jnp.int32),
            pltpu.VMEM((3, 4), F32),
            pltpu.VMEM((64, 16, LANES), F32),
            pltpu.SemaphoreType.DMA((5,)),
            pltpu.SemaphoreType.DMA((4,)),
        ),
    )
    state = exchange(state, ["y", "zh", "zl", "c"]).reshape(1024, LANES)
    gates, factors = call(kernel_tables, "tables", TABLES, *shared)
    kept, soon, later = call(
        kernel_b,
        "second_gates",
        [jax.ShapeDtypeStruct(shape, F32) for shape in ((4, 128, 128), (128, 128), (3, 128, 128))],
        state,
        gates,
        factors,
    )
    soon = from_partner(soon, "c", 1)
    later = from_partner(later, "c", 1)
    got = {1: later[1], 2: soon, 3: later[2]}
    arrived = {k: from_partner(jnp.stack([kept[k], got[k]]), "x", k) for k in (2, 3, 1)}
    got = later
    state = call(
        kernel_c, "third_gates", shape, kept, got, arrived[2], arrived[3], arrived[1], gates, factors
    )
    state = exchange(state, ["zh", "zl", "y", "c", "x"])
    state = call(
        kernel_d,
        "last_gate",
        shape,
        state,
        gates,
        out_space=HBM,
        scratch=(pltpu.VMEM((1024, LANES), F32), pltpu.SemaphoreType.DMA((2,))),
    )
    return state.reshape(512, 2, LANES).transpose(1, 0, 2).reshape(2, 65536)


def solution(mesh):
    return jax.shard_map(
        body,
        mesh=mesh,
        in_specs=(P(None, AXES), P(), P(), P(), P()),
        out_specs=P(None, AXES),
        check_vma=False,
    )
```

```python
import itertools

import jax
import jax.numpy as jnp
from jax import lax
from jax.experimental import pallas as pl
from jax.experimental.pallas import tpu as pltpu
from jax.sharding import PartitionSpec as P

AXES = ("qa", "qb")
SIZES = {"y": 4, "zl": 4, "c": 2, "zh": 2, "x": 4}
F32 = jnp.float32
BF16 = jnp.bfloat16
LANES = 128


def device_groups(varying):
    fixed = [name for name in SIZES if name not in varying]
    groups = []
    for held in itertools.product(*[range(SIZES[name]) for name in fixed]):
        group = []
        for moved in itertools.product(*[range(SIZES[name]) for name in varying]):
            at = dict(zip(fixed, held)) | dict(zip(varying, moved))
            group.append((at["y"] * 8 + at["zl"] * 2 + at["c"]) * 8 + at["zh"] * 4 + at["x"])
        groups.append(group)
    return groups


def exchange(values, varying):
    groups = device_groups(varying)
    parts = values.reshape(len(groups[0]), -1, LANES)
    moved = lax.all_to_all(parts, AXES, 0, 0, axis_index_groups=groups, tiled=True)
    return moved.reshape(values.shape)


def from_partner(value, varying, mask):
    pairs = [
        (group[at], group[at ^ mask]) for group in device_groups([varying]) for at in range(len(group))
    ]
    return lax.ppermute(value, AXES, pairs)


def iota(axis, shape=(128, 128)):
    return lax.broadcasted_iota(jnp.int32, shape, axis)


def take_bits(index, places):
    total = None
    for source, place in enumerate(places):
        bit = jnp.left_shift(jnp.bitwise_and(jnp.right_shift(index, source), 1), place)
        total = bit if total is None else total + bit
    return total


def onehot(order_ref, gate, index):
    mapped = None
    order = order_ref[...]
    for target in range(7):
        shift = order[gate : gate + 1, target : target + 1]
        bit = jnp.bitwise_and(jnp.right_shift(index, shift), 1)
        bit = jnp.left_shift(bit, target)
        mapped = bit if mapped is None else mapped + bit
    return (mapped == iota(1)).astype(F32).astype(BF16)


def mul(left, right):
    return jnp.dot(left, right, preferred_element_type=F32)


def mul_t(left, right):
    return lax.dot_general(left, right, (((1,), (1,)), ((), ())), preferred_element_type=F32)


def halves(values):
    high = values.astype(BF16)
    return high, (values - high.astype(F32)).astype(BF16)


def gate_block(mats, order_ref, gate, rows=None, columns=None):
    rows = onehot(order_ref, gate, iota(0) if rows is None else rows)
    columns = rows if columns is None else onehot(order_ref, gate, columns)
    parts = [half for part in range(2) for half in halves(mats[part])]
    turned = mul_t(columns, jnp.concatenate(parts, axis=0)).astype(BF16)
    parts = [mul_t(rows, turned[:, at * 128 : (at + 1) * 128]).astype(BF16) for at in range(4)]
    return [(parts[0], parts[2]), (parts[1], parts[3])]


def full_block(blocks):
    out = []
    for vr, vi in blocks:
        out.append(
            jnp.concatenate(
                [jnp.concatenate([vr, -vi], axis=1), jnp.concatenate([vi, vr], axis=1)], axis=0
            )
        )
    return out


def thrice(high, low):
    return jnp.concatenate([high, high, low], axis=1)


def product(multiply, block, values, values_left=False):
    high, low = halves(values)
    values = jnp.concatenate([high, low, high], axis=0 if multiply is mul else 1)
    return multiply(values, block) if values_left else multiply(block, values)


def sign_of(index, pairs, layer, term):
    first = jnp.right_shift(index, pairs[layer, 0:1, term : term + 1])
    second = jnp.right_shift(index, pairs[layer, 1:2, term : term + 1])
    bit = jnp.bitwise_and(jnp.bitwise_xor(first, second), 1)
    return (1 - 2 * bit).astype(F32)


class Phase:
    def __init__(self, pairs_ref, angles_ref, layer, index):
        self.pairs = pairs_ref[...]
        self.layer = layer
        angles = angles_ref[...]
        cosine = jnp.cos(angles)
        sine = jnp.sin(angles)
        self.cosine = [cosine[layer : layer + 1, term : term + 1] for term in range(4)]
        self.sine = [
            sine[layer : layer + 1, term : term + 1] * sign_of(index, self.pairs, layer, term)
            for term in range(4)
        ]

    def factor(self, rest):
        rest = jnp.full((1, 1), rest, jnp.int32)
        factors = []
        for term in range(4):
            sign = sign_of(rest, self.pairs, self.layer, term)
            factors.append((self.cosine[term], self.sine[term] * sign))

        def pair(first, second):
            return (
                first[0] * second[0] - first[1] * second[1],
                first[0] * second[1] + first[1] * second[0],
            )

        return pair(pair(factors[0], factors[1]), pair(factors[2], factors[3]))


def rotate(factor, real, imag):
    cosine, sine = factor
    return real * cosine - imag * sine, real * sine + imag * cosine


def swap_bit(tiles, tile_bit, lane_bit):
    width = 1 << lane_bit
    lane = iota(1, tiles[0].shape)
    low = jnp.bitwise_and(lane, width) == 0
    out = list(tiles)
    for number in range(len(tiles)):
        other = number | (1 << tile_bit)
        if other == number:
            continue
        first, second = tiles[number], tiles[other]
        if 2 * width == LANES:
            moved = pltpu.roll(jnp.where(low, second, first), width, 1)
            out[number] = jnp.where(low, first, moved)
            out[other] = jnp.where(low, moved, second)
            continue
        out[number] = jnp.where(low, first, pltpu.roll(second, width, 1))
        out[other] = jnp.where(low, pltpu.roll(first, LANES - width, 1), second)
    return out


def place():
    qa = lax.axis_index("qa")
    qb = lax.axis_index("qb")
    return qa // 8, qa // 2 % 4, qa % 2, qb // 4, qb % 4


def kernel_a(
    amps_hbm, mats_hbm, order_hbm, pairs_hbm, angles_hbm, out_hbm,
    amps, mats, order, pairs, angles, out, sems, out_sems,
):
    sources = (mats_hbm.at[1], order_hbm, pairs_hbm, angles_hbm, amps_hbm)
    targets = (mats, order, pairs, angles, amps)
    copies = [
        pltpu.make_async_copy(source, target, sems.at[number])
        for number, (source, target) in enumerate(zip(sources, targets))
    ]
    for copy in copies:
        copy.start()
    for copy in copies[:4]:
        copy.wait()
    block = thrice(*full_block(gate_block(mats, order, 1)))
    y, zl, core, zh, x = place()
    device = y * (1 << 22) + zl * (1 << 20) + core * (1 << 19) + zh * (1 << 18) + x * (1 << 16)
    phase = Phase(pairs, angles, 0, iota(0) * 512 + iota(1))
    copies[4].wait()
    written = []
    for mid in range(4):
        real = amps[pl.ds(2 * mid, 128, stride=8), :]
        imag = amps[pl.ds(2 * mid + 1, 128, stride=8), :]
        real, imag = rotate(phase.factor(device + mid * 128), real, imag)
        values = jnp.concatenate([real, imag], axis=1)
        result = product(mul_t, block, values)
        for part in range(2):
            tiles = result[part * 128 : (part + 1) * 128].reshape(16, 8, LANES)
            out[mid * 16 : (mid + 1) * 16, part * 8 : (part + 1) * 8, :] = tiles
        piece = pl.ds(mid * 16, 16)
        written.append(pltpu.make_async_copy(out.at[piece], out_hbm.at[piece], out_sems.at[mid]))
        written[-1].start()
    for copy in written:
        copy.wait()


def kernel_tables(mats_ref, order_ref, pairs_ref, angles_ref, gates_ref, factors_ref):
    y, zl, core, zh, x = place()
    held = y * (1 << 7) + zh * (1 << 6) + zl * (1 << 4)
    row, lane = iota(0), iota(1)
    index = (row // 32) * (1 << 14) + (row % 32) * (1 << 19) + (lane // 32) + (lane % 32) * 512
    phase = Phase(pairs_ref, angles_ref, 1, index)
    device = held + core * (1 << 3) + x * (1 << 16)
    for u in range(4):
        factor = phase.factor(device + (u // 2) * (1 << 18) + (u % 2) * 4)
        for part in range(2):
            factors_ref[0, part, u] = factor[part]
    index = (row // 16) * (1 << 16) + (row % 16) + (lane // 32) * (1 << 14) + (lane % 32) * (1 << 19)
    phase = Phase(pairs_ref, angles_ref, 2, index)
    device = held + core * (1 << 11) + x * (1 << 9)
    for xl in range(4):
        factor = phase.factor(device + xl * (1 << 12))
        for part in range(2):
            factors_ref[1, part, xl] = factor[part]
    natural = iota(0)
    arrived = take_bits(natural, (0, 1, 2, 6, 3, 4, 5))
    leaving = take_bits(natural, (0, 3, 4, 1, 2, 5, 6))
    for slot, gate in enumerate((0, 3, 2, 4, 5)):
        rows = columns = natural
        if gate == 3:
            rows = take_bits(natural, (3, 4, 0, 1, 2, 5, 6)) ^ (core * 4 + x)
        if gate == 2:
            columns = arrived ^ (x * 16 + core * 8)
        if gate == 4:
            rows = leaving
        blocks = gate_block(
            mats_ref.at[gate], order_ref, gate, rows, None if rows is columns else columns
        )
        block = thrice(*full_block(blocks))
        if gate == 3:
            block = block.astype(F32).reshape(2, 32, 4, 768)
            block = jnp.concatenate([block[0], block[1]], axis=1).reshape(256, 768).astype(BF16)
        gates_ref[slot] = block


def kernel_b(amps_ref, gates_ref, factors_ref, kept_ref, soon_ref, later_ref):
    for first in range(0, 4, 2):
        group = range(first, first + 2)
        columns = []
        for u in group:
            parts = []
            for part in range(2):
                start = (u // 2) * 128 + part * 8 + (u % 2) * 4
                tiles = [
                    jnp.concatenate(
                        [amps_ref[pl.ds(y * 256 + start + t, 8, stride=16), :] for y in range(4)], axis=0
                    )
                    for t in range(4)
                ]
                tiles = swap_bit(swap_bit(tiles, 1, 6), 0, 5)
                parts += tiles
            columns.append(jnp.concatenate(parts, axis=0))
        result = product(mul, gates_ref[0], jnp.concatenate(columns, axis=1))
        rows = []
        for at, u in enumerate(group):
            real = result[:128, at * 128 : (at + 1) * 128]
            imag = result[128:, at * 128 : (at + 1) * 128]
            parts = []
            for value in rotate((factors_ref[0, 0, u], factors_ref[0, 1, u]), real, imag):
                tiles = [value[ah * 32 : (ah + 1) * 32] for ah in range(4)]
                tiles = swap_bit(swap_bit(tiles, 1, 6), 0, 5)
                parts.append(jnp.concatenate(tiles, axis=0))
            rows.append(jnp.concatenate(parts, axis=1))
        result = product(mul_t, gates_ref[1], jnp.concatenate(rows, axis=0))
        for at, u in enumerate(group):
            values = result[:, at * 128 : (at + 1) * 128]
            tiles = [values[ah * 64 : (ah + 1) * 64] for ah in range(4)]
            tiles = swap_bit(swap_bit(tiles, 1, 6), 0, 5)
            for t in range(4):
                to = (u * 4 + t) * 8
                for k in range(4):
                    kept_ref[k, to : to + 8, :] = tiles[t][k * 8 : k * 8 + 8]
                    if k == 2:
                        soon_ref[to : to + 8, :] = tiles[t][k * 8 + 32 : k * 8 + 40]
                    else:
                        later_ref[min(k, 2), to : to + 8, :] = tiles[t][k * 8 + 32 : k * 8 + 40]


def kernel_c(kept_ref, got_ref, *refs):
    arrived, (gates_ref, factors_ref, out_ref) = refs[:3], refs[3:]
    rotated = []
    for start in range(0, 4, 2):
        columns = []
        for xl in range(start, start + 2):
            parts = []
            for part in range(2):
                rows = pl.ds(part * 4 + xl, 16, stride=8)
                parts += [kept_ref[0, rows, :], got_ref[0, rows, :]]
                for ref in (arrived[2], arrived[0], arrived[1]):
                    parts += [ref[0, rows, :], ref[1, rows, :]]
            columns.append(jnp.concatenate(parts, axis=0))
        result = product(mul, gates_ref[2], jnp.concatenate(columns, axis=1))
        for at in range(2):
            rotated.append(
                rotate(
                    (factors_ref[1, 0, start + at], factors_ref[1, 1, start + at]),
                    result[:128, at * 128 : (at + 1) * 128],
                    result[128:, at * 128 : (at + 1) * 128],
                )
            )
    for start in range(0, 4, 2):
        rows = []
        for gb in range(2 * start, 2 * (start + 2)):
            for real, imag in rotated:
                at = slice(gb * 16, (gb + 1) * 16)
                rows.append(jnp.concatenate([real[at], imag[at]], axis=1))
        result = product(mul_t, gates_ref[3], jnp.concatenate(rows, axis=0))
        for pair in range(start, start + 2):
            values = result[:, (pair - start) * 128 : (pair - start + 1) * 128]
            tiles = swap_bit([values[:128], values[128:]], 0, 6)
            for last in range(2):
                start_row = (pair // 2) * 512 + (pair % 2 * 2 + last) * 4
                for ah in range(4):
                    rows = pl.ds(start_row + ah, 32, stride=16)
                    out_ref[rows, :] = tiles[last][ah * 32 : (ah + 1) * 32]


def kernel_d(amps_ref, gates_ref, out_hbm, out, sems):
    written = []
    for half in range(2):
        rows = []
        for ah in range(half * 2, half * 2 + 2):
            for mid in range(4):
                tiles = [
                    amps_ref[pl.ds(xb * 128 + mid * 32 + ah, 8, stride=4), :] for xb in range(8)
                ]
                tiles = swap_bit(swap_bit(swap_bit(tiles, 2, 6), 1, 5), 0, 4)
                for xl in range(4):
                    rows.append(jnp.concatenate([tiles[xl], tiles[4 + xl]], axis=1))
        result = product(mul_t, gates_ref[4], jnp.concatenate(rows, axis=0), values_left=True)
        for at, (ah, mid, xl) in enumerate(itertools.product(range(2), range(4), range(4))):
            to = (half * 2 + ah) * 128 + xl * 32 + mid
            for part in range(2):
                out[pl.ds(2 * to + part, 8, stride=8), :] = result[
                    at * 8 : at * 8 + 8, part * 128 : (part + 1) * 128
                ]
        piece = pl.ds(half * 512, 512)
        written.append(pltpu.make_async_copy(out.at[piece], out_hbm.at[piece], sems.at[half]))
        written[-1].start()
    for copy in written:
        copy.wait()


VMEM = pl.BlockSpec(memory_space=pltpu.VMEM)
HBM = pl.BlockSpec(memory_space=pltpu.HBM)
TABLES = (
    jax.ShapeDtypeStruct((5, 256, 768), BF16),
    jax.ShapeDtypeStruct((2, 2, 4, 128, LANES), F32),
)


def call(kernel, name, out_shape, *operands, space=VMEM, out_space=VMEM, scratch=(), mib=24):
    return pl.pallas_call(
        kernel,
        out_shape=out_shape,
        in_specs=[space] * len(operands),
        out_specs=jax.tree.map(lambda _: out_space, out_shape),
        scratch_shapes=list(scratch),
        compiler_params=pltpu.CompilerParams(vmem_limit_bytes=mib * 1024 * 1024),
        cost_estimate=pl.CostEstimate(flops=400_000_000, bytes_accessed=2_000_000, transcendentals=0),
        name=name,
    )(*operands)


def body(amplitudes, gate_mats, gate_order, phase_pairs, phase_angles):
    pairs = phase_pairs.transpose(0, 2, 1)
    shared = (gate_mats, gate_order, pairs, phase_angles)
    shape = jax.ShapeDtypeStruct((1024, LANES), F32)
    state = amplitudes.reshape(2, 512, LANES).transpose(1, 0, 2).reshape(1024, LANES)
    state = call(
        kernel_a,
        "first_gate",
        jax.ShapeDtypeStruct((64, 16, LANES), F32),
        state,
        *shared,
        space=HBM,
        out_space=HBM,
        mib=63,
        scratch=(
            pltpu.VMEM((1024, LANES), F32),
            pltpu.VMEM((2, 128, LANES), F32),
            pltpu.VMEM((6, 7), jnp.int32),
            pltpu.VMEM((3, 2, 4), jnp.int32),
            pltpu.VMEM((3, 4), F32),
            pltpu.VMEM((64, 16, LANES), F32),
            pltpu.SemaphoreType.DMA((5,)),
            pltpu.SemaphoreType.DMA((4,)),
        ),
    )
    state = exchange(state, ["y", "zh", "zl", "c"]).reshape(1024, LANES)
    gates, factors = call(kernel_tables, "tables", TABLES, *shared)
    kept, soon, later = call(
        kernel_b,
        "second_gates",
        [jax.ShapeDtypeStruct(shape, F32) for shape in ((4, 128, 128), (128, 128), (3, 128, 128))],
        state,
        gates,
        factors,
    )
    soon = from_partner(soon, "c", 1)
    later = from_partner(later, "c", 1)
    got = {1: later[1], 2: soon, 3: later[2]}
    arrived = {k: from_partner(jnp.stack([kept[k], got[k]]), "x", k) for k in (2, 3, 1)}
    got = later
    state = call(
        kernel_c, "third_gates", shape, kept, got, arrived[2], arrived[3], arrived[1], gates, factors
    )
    state = exchange(state, ["zh", "zl", "y", "c", "x"])
    state = call(
        kernel_d,
        "last_gate",
        shape,
        state,
        gates,
        out_space=HBM,
        scratch=(pltpu.VMEM((1024, LANES), F32), pltpu.SemaphoreType.DMA((2,))),
    )
    return state.reshape(512, 2, LANES).transpose(1, 0, 2).reshape(2, 65536)


def solution(mesh):
    return jax.shard_map(
        body,
        mesh=mesh,
        in_specs=(P(None, AXES), P(), P(), P(), P()),
        out_specs=P(None, AXES),
        check_vma=False,
    )
```

```python
import itertools

import jax
import jax.numpy as jnp
from jax import lax
from jax.experimental import pallas as pl
from jax.experimental.pallas import tpu as pltpu
from jax.sharding import PartitionSpec as P

AXES = ("qa", "qb")
SIZES = {"y": 4, "zl": 4, "c": 2, "zh": 2, "x": 4}
F32 = jnp.float32
BF16 = jnp.bfloat16
LANES = 128


def device_groups(varying):
    fixed = [name for name in SIZES if name not in varying]
    groups = []
    for held in itertools.product(*[range(SIZES[name]) for name in fixed]):
        group = []
        for moved in itertools.product(*[range(SIZES[name]) for name in varying]):
            at = dict(zip(fixed, held)) | dict(zip(varying, moved))
            group.append((at["y"] * 8 + at["zl"] * 2 + at["c"]) * 8 + at["zh"] * 4 + at["x"])
        groups.append(group)
    return groups


def exchange(values, varying):
    groups = device_groups(varying)
    parts = values.reshape(len(groups[0]), -1, LANES)
    moved = lax.all_to_all(parts, AXES, 0, 0, axis_index_groups=groups, tiled=True)
    return moved.reshape(values.shape)


def from_partner(value, varying, mask):
    pairs = [
        (group[at], group[at ^ mask]) for group in device_groups([varying]) for at in range(len(group))
    ]
    return lax.ppermute(value, AXES, pairs)


def iota(axis, shape=(128, 128)):
    return lax.broadcasted_iota(jnp.int32, shape, axis)


def take_bits(index, places):
    total = None
    for source, place in enumerate(places):
        bit = jnp.left_shift(jnp.bitwise_and(jnp.right_shift(index, source), 1), place)
        total = bit if total is None else total + bit
    return total


def onehot(order_ref, gate, index):
    mapped = None
    order = order_ref[...]
    for target in range(7):
        shift = order[gate : gate + 1, target : target + 1]
        bit = jnp.bitwise_and(jnp.right_shift(index, shift), 1)
        bit = jnp.left_shift(bit, target)
        mapped = bit if mapped is None else mapped + bit
    return (mapped == iota(1)).astype(F32).astype(BF16)


def mul(left, right):
    return jnp.dot(left, right, preferred_element_type=F32)


def mul_t(left, right):
    return lax.dot_general(left, right, (((1,), (1,)), ((), ())), preferred_element_type=F32)


def halves(values):
    high = values.astype(BF16)
    return high, (values - high.astype(F32)).astype(BF16)


def gate_block(mats, order_ref, gate, rows=None, columns=None):
    rows = onehot(order_ref, gate, iota(0) if rows is None else rows)
    columns = rows if columns is None else onehot(order_ref, gate, columns)
    parts = [half for part in range(2) for half in halves(mats[part])]
    turned = mul_t(columns, jnp.concatenate(parts, axis=0)).astype(BF16)
    parts = [mul_t(rows, turned[:, at * 128 : (at + 1) * 128]).astype(BF16) for at in range(4)]
    return [(parts[0], parts[2]), (parts[1], parts[3])]


def full_block(blocks):
    out = []
    for vr, vi in blocks:
        out.append(
            jnp.concatenate(
                [jnp.concatenate([vr, -vi], axis=1), jnp.concatenate([vi, vr], axis=1)], axis=0
            )
        )
    return out


def thrice(high, low):
    return jnp.concatenate([high, high, low], axis=1)


def product(multiply, block, values, values_left=False):
    high, low = halves(values)
    values = jnp.concatenate([high, low, high], axis=0 if multiply is mul else 1)
    return multiply(values, block) if values_left else multiply(block, values)


def sign_of(index, pairs, layer, term):
    first = jnp.right_shift(index, pairs[layer, 0:1, term : term + 1])
    second = jnp.right_shift(index, pairs[layer, 1:2, term : term + 1])
    bit = jnp.bitwise_and(jnp.bitwise_xor(first, second), 1)
    return (1 - 2 * bit).astype(F32)


class Phase:
    def __init__(self, pairs_ref, angles_ref, layer, index):
        self.pairs = pairs_ref[...]
        self.layer = layer
        angles = angles_ref[...]
        cosine = jnp.cos(angles)
        sine = jnp.sin(angles)
        self.cosine = [cosine[layer : layer + 1, term : term + 1] for term in range(4)]
        self.sine = [
            sine[layer : layer + 1, term : term + 1] * sign_of(index, self.pairs, layer, term)
            for term in range(4)
        ]

    def factor(self, rest):
        rest = jnp.full((1, 1), rest, jnp.int32)
        factors = []
        for term in range(4):
            sign = sign_of(rest, self.pairs, self.layer, term)
            factors.append((self.cosine[term], self.sine[term] * sign))

        def pair(first, second):
            return (
                first[0] * second[0] - first[1] * second[1],
                first[0] * second[1] + first[1] * second[0],
            )

        return pair(pair(factors[0], factors[1]), pair(factors[2], factors[3]))


def rotate(factor, real, imag):
    cosine, sine = factor
    return real * cosine - imag * sine, real * sine + imag * cosine


def swap_bit(tiles, tile_bit, lane_bit):
    width = 1 << lane_bit
    lane = iota(1, tiles[0].shape)
    low = jnp.bitwise_and(lane, width) == 0
    out = list(tiles)
    for number in range(len(tiles)):
        other = number | (1 << tile_bit)
        if other == number:
            continue
        first, second = tiles[number], tiles[other]
        if 2 * width == LANES:
            moved = pltpu.roll(jnp.where(low, second, first), width, 1)
            out[number] = jnp.where(low, first, moved)
            out[other] = jnp.where(low, moved, second)
            continue
        out[number] = jnp.where(low, first, pltpu.roll(second, width, 1))
        out[other] = jnp.where(low, pltpu.roll(first, LANES - width, 1), second)
    return out


def place():
    qa = lax.axis_index("qa")
    qb = lax.axis_index("qb")
    return qa // 8, qa // 2 % 4, qa % 2, qb // 4, qb % 4


def kernel_a(
    amps_hbm, mats_hbm, order_hbm, pairs_hbm, angles_hbm, out_hbm,
    amps, mats, order, pairs, angles, out, sems, out_sems,
):
    sources = (mats_hbm.at[1], order_hbm, pairs_hbm, angles_hbm, amps_hbm)
    targets = (mats, order, pairs, angles, amps)
    copies = [
        pltpu.make_async_copy(source, target, sems.at[number])
        for number, (source, target) in enumerate(zip(sources, targets))
    ]
    for copy in copies:
        copy.start()
    for copy in copies[:4]:
        copy.wait()
    block = thrice(*full_block(gate_block(mats, order, 1)))
    y, zl, core, zh, x = place()
    device = y * (1 << 22) + zl * (1 << 20) + core * (1 << 19) + zh * (1 << 18) + x * (1 << 16)
    phase = Phase(pairs, angles, 0, iota(0) * 512 + iota(1))
    copies[4].wait()
    written = []
    for mid in range(4):
        real = amps[pl.ds(2 * mid, 128, stride=8), :]
        imag = amps[pl.ds(2 * mid + 1, 128, stride=8), :]
        real, imag = rotate(phase.factor(device + mid * 128), real, imag)
        values = jnp.concatenate([real, imag], axis=1)
        result = product(mul_t, block, values)
        for part in range(2):
            tiles = result[part * 128 : (part + 1) * 128].reshape(16, 8, LANES)
            out[mid * 16 : (mid + 1) * 16, part * 8 : (part + 1) * 8, :] = tiles
        piece = pl.ds(mid * 16, 16)
        written.append(pltpu.make_async_copy(out.at[piece], out_hbm.at[piece], out_sems.at[mid]))
        written[-1].start()
    for copy in written:
        copy.wait()


def kernel_tables(mats_ref, order_ref, pairs_ref, angles_ref, gates_ref, factors_ref):
    y, zl, core, zh, x = place()
    held = y * (1 << 7) + zh * (1 << 6) + zl * (1 << 4)
    row, lane = iota(0), iota(1)
    index = (row // 32) * (1 << 14) + (row % 32) * (1 << 19) + (lane // 32) + (lane % 32) * 512
    phase = Phase(pairs_ref, angles_ref, 1, index)
    device = held + core * (1 << 3) + x * (1 << 16)
    for u in range(4):
        factor = phase.factor(device + (u // 2) * (1 << 18) + (u % 2) * 4)
        for part in range(2):
            factors_ref[0, part, u] = factor[part]
    index = (row // 16) * (1 << 16) + (row % 16) + (lane // 32) * (1 << 14) + (lane % 32) * (1 << 19)
    phase = Phase(pairs_ref, angles_ref, 2, index)
    device = held + core * (1 << 11) + x * (1 << 9)
    for xl in range(4):
        factor = phase.factor(device + xl * (1 << 12))
        for part in range(2):
            factors_ref[1, part, xl] = factor[part]
    natural = iota(0)
    arrived = take_bits(natural, (0, 1, 2, 6, 3, 5, 4))
    leaving = take_bits(natural, (0, 3, 4, 1, 2, 5, 6))
    for slot, gate in enumerate((0, 3, 2, 4, 5)):
        rows = columns = natural
        if gate == 3:
            rows = take_bits(natural, (3, 4, 0, 1, 2, 5, 6)) ^ (core * 4 + x)
        if gate == 2:
            columns = arrived ^ (x * 16 + core * 8)
        if gate == 4:
            rows = leaving
        blocks = gate_block(
            mats_ref.at[gate], order_ref, gate, rows, None if rows is columns else columns
        )
        full = full_block(blocks)
        block = thrice(*full)
        if gate == 2:
            full = [half.astype(F32) for half in full]
            early = [jnp.concatenate([half[:, :64], half[:, 128:192]], axis=1) for half in full]
            late = [jnp.concatenate([half[:, 64:128], half[:, 192:]], axis=1) for half in full]
            block = jnp.concatenate([thrice(*early), thrice(*late)], axis=1).astype(BF16)
        if gate == 3:
            block = block.astype(F32).reshape(2, 32, 4, 768)
            block = jnp.concatenate([block[0], block[1]], axis=1).reshape(256, 768).astype(BF16)
        gates_ref[slot] = block


def kernel_b(amps_ref, gates_ref, factors_ref, kept_ref, soon_ref, later_ref):
    for first in range(0, 4, 2):
        group = range(first, first + 2)
        columns = []
        for u in group:
            parts = []
            for part in range(2):
                start = (u // 2) * 128 + part * 8 + (u % 2) * 4
                tiles = [
                    jnp.concatenate(
                        [amps_ref[pl.ds(y * 256 + start + t, 8, stride=16), :] for y in range(4)], axis=0
                    )
                    for t in range(4)
                ]
                tiles = swap_bit(swap_bit(tiles, 1, 6), 0, 5)
                parts += tiles
            columns.append(jnp.concatenate(parts, axis=0))
        result = product(mul, gates_ref[0], jnp.concatenate(columns, axis=1))
        rows = []
        for at, u in enumerate(group):
            real = result[:128, at * 128 : (at + 1) * 128]
            imag = result[128:, at * 128 : (at + 1) * 128]
            parts = []
            for value in rotate((factors_ref[0, 0, u], factors_ref[0, 1, u]), real, imag):
                tiles = [value[ah * 32 : (ah + 1) * 32] for ah in range(4)]
                tiles = swap_bit(swap_bit(tiles, 1, 6), 0, 5)
                parts.append(jnp.concatenate(tiles, axis=0))
            rows.append(jnp.concatenate(parts, axis=1))
        result = product(mul_t, gates_ref[1], jnp.concatenate(rows, axis=0))
        for at, u in enumerate(group):
            values = result[:, at * 128 : (at + 1) * 128]
            tiles = [values[ah * 64 : (ah + 1) * 64] for ah in range(4)]
            tiles = swap_bit(swap_bit(tiles, 1, 6), 0, 5)
            for t in range(4):
                to = (u * 4 + t) * 8
                for k in range(4):
                    kept_ref[k, to : to + 8, :] = tiles[t][k * 8 : k * 8 + 8]
                    if k == 2:
                        soon_ref[to : to + 8, :] = tiles[t][k * 8 + 32 : k * 8 + 40]
                    else:
                        later_ref[min(k, 2), to : to + 8, :] = tiles[t][k * 8 + 32 : k * 8 + 40]


def some_rows(refs, xl):
    parts = []
    for part in range(2):
        rows = pl.ds(part * 4 + xl, 16, stride=8)
        for ref, at in refs:
            parts.append(ref[at, rows, :])
    return jnp.concatenate(parts, axis=0)


def kernel_c1(kept_ref, got_ref, second_ref, gates_ref, out_ref):
    refs = ((kept_ref, 0), (got_ref, 0), (second_ref, 0), (second_ref, 1))
    for start in range(0, 4, 2):
        columns = [some_rows(refs, xl) for xl in range(start, start + 2)]
        lanes = slice(start * 128, (start + 2) * 128)
        out_ref[:, lanes] = product(mul, gates_ref[2, :, :384], jnp.concatenate(columns, axis=1))


def kernel_c(sum_ref, third_ref, first_ref, gates_ref, factors_ref, out_ref):
    refs = ((first_ref, 0), (first_ref, 1), (third_ref, 0), (third_ref, 1))
    rotated = []
    for start in range(0, 4, 2):
        columns = [some_rows(refs, xl) for xl in range(start, start + 2)]
        lanes = slice(start * 128, (start + 2) * 128)
        result = product(mul, gates_ref[2, :, 384:], jnp.concatenate(columns, axis=1))
        result = result + sum_ref[:, lanes]
        for at in range(2):
            rotated.append(
                rotate(
                    (factors_ref[1, 0, start + at], factors_ref[1, 1, start + at]),
                    result[:128, at * 128 : (at + 1) * 128],
                    result[128:, at * 128 : (at + 1) * 128],
                )
            )
    for start in range(0, 4, 2):
        rows = []
        for gb in range(2 * start, 2 * (start + 2)):
            for real, imag in rotated:
                at = slice(gb * 16, (gb + 1) * 16)
                rows.append(jnp.concatenate([real[at], imag[at]], axis=1))
        result = product(mul_t, gates_ref[3], jnp.concatenate(rows, axis=0))
        for pair in range(start, start + 2):
            values = result[:, (pair - start) * 128 : (pair - start + 1) * 128]
            tiles = swap_bit([values[:128], values[128:]], 0, 6)
            for last in range(2):
                start_row = (pair // 2) * 512 + (pair % 2 * 2 + last) * 4
                for ah in range(4):
                    rows = pl.ds(start_row + ah, 32, stride=16)
                    out_ref[rows, :] = tiles[last][ah * 32 : (ah + 1) * 32]


def kernel_d(amps_ref, gates_ref, out_hbm, out, sems):
    written = []
    for half in range(2):
        rows = []
        for ah in range(half * 2, half * 2 + 2):
            for mid in range(4):
                tiles = [
                    amps_ref[pl.ds(xb * 128 + mid * 32 + ah, 8, stride=4), :] for xb in range(8)
                ]
                tiles = swap_bit(swap_bit(swap_bit(tiles, 2, 6), 1, 5), 0, 4)
                for xl in range(4):
                    rows.append(jnp.concatenate([tiles[xl], tiles[4 + xl]], axis=1))
        result = product(mul_t, gates_ref[4], jnp.concatenate(rows, axis=0), values_left=True)
        for at, (ah, mid, xl) in enumerate(itertools.product(range(2), range(4), range(4))):
            to = (half * 2 + ah) * 128 + xl * 32 + mid
            for part in range(2):
                out[pl.ds(2 * to + part, 8, stride=8), :] = result[
                    at * 8 : at * 8 + 8, part * 128 : (part + 1) * 128
                ]
        piece = pl.ds(half * 512, 512)
        written.append(pltpu.make_async_copy(out.at[piece], out_hbm.at[piece], sems.at[half]))
        written[-1].start()
    for copy in written:
        copy.wait()


VMEM = pl.BlockSpec(memory_space=pltpu.VMEM)
HBM = pl.BlockSpec(memory_space=pltpu.HBM)
TABLES = (
    jax.ShapeDtypeStruct((5, 256, 768), BF16),
    jax.ShapeDtypeStruct((2, 2, 4, 128, LANES), F32),
)


def call(kernel, name, out_shape, *operands, space=VMEM, out_space=VMEM, scratch=(), mib=24):
    return pl.pallas_call(
        kernel,
        out_shape=out_shape,
        in_specs=[space] * len(operands),
        out_specs=jax.tree.map(lambda _: out_space, out_shape),
        scratch_shapes=list(scratch),
        compiler_params=pltpu.CompilerParams(vmem_limit_bytes=mib * 1024 * 1024),
        cost_estimate=pl.CostEstimate(flops=400_000_000, bytes_accessed=2_000_000, transcendentals=0),
        name=name,
    )(*operands)


def body(amplitudes, gate_mats, gate_order, phase_pairs, phase_angles):
    pairs = phase_pairs.transpose(0, 2, 1)
    shared = (gate_mats, gate_order, pairs, phase_angles)
    shape = jax.ShapeDtypeStruct((1024, LANES), F32)
    state = amplitudes.reshape(2, 512, LANES).transpose(1, 0, 2).reshape(1024, LANES)
    state = call(
        kernel_a,
        "first_gate",
        jax.ShapeDtypeStruct((64, 16, LANES), F32),
        state,
        *shared,
        space=HBM,
        out_space=HBM,
        mib=63,
        scratch=(
            pltpu.VMEM((1024, LANES), F32),
            pltpu.VMEM((2, 128, LANES), F32),
            pltpu.VMEM((6, 7), jnp.int32),
            pltpu.VMEM((3, 2, 4), jnp.int32),
            pltpu.VMEM((3, 4), F32),
            pltpu.VMEM((64, 16, LANES), F32),
            pltpu.SemaphoreType.DMA((5,)),
            pltpu.SemaphoreType.DMA((4,)),
        ),
    )
    state = exchange(state, ["y", "zh", "zl", "c"]).reshape(1024, LANES)
    gates, factors = call(kernel_tables, "tables", TABLES, *shared)
    kept, soon, later = call(
        kernel_b,
        "second_gates",
        [jax.ShapeDtypeStruct(shape, F32) for shape in ((4, 128, 128), (128, 128), (3, 128, 128))],
        state,
        gates,
        factors,
    )
    soon = from_partner(soon, "c", 1)
    later = from_partner(later, "c", 1)
    got = {1: later[1], 2: soon, 3: later[2]}
    arrived = {k: from_partner(jnp.stack([kept[k], got[k]]), "x", k) for k in (2, 3, 1)}
    got = later
    total = call(
        kernel_c1,
        "third_gates_early",
        jax.ShapeDtypeStruct((256, 512), F32),
        kept,
        got,
        arrived[2],
        gates,
    )
    state = call(kernel_c, "third_gates", shape, total, arrived[3], arrived[1], gates, factors)
    state = exchange(state, ["zh", "zl", "y", "c", "x"])
    state = call(
        kernel_d,
        "last_gate",
        shape,
        state,
        gates,
        out_space=HBM,
        scratch=(pltpu.VMEM((1024, LANES), F32), pltpu.SemaphoreType.DMA((2,))),
    )
    return state.reshape(512, 2, LANES).transpose(1, 0, 2).reshape(2, 65536)


def solution(mesh):
    return jax.shard_map(
        body,
        mesh=mesh,
        in_specs=(P(None, AXES), P(), P(), P(), P()),
        out_specs=P(None, AXES),
        check_vma=False,
    )
```
